32 devices in a mesh: freq: 16 (over z, x, core), beam: 2 (over y).
Axes of the slice: x: 2, y: 2, z: 4, core: 2. Of those that a mesh axis runs over, the one named last changes fastest.
Arguments:
- voltages: bfloat16 [2, 4, 1024, 16, 256], P(None, 'beam', 'freq'), parts along dimension 1, may hold values from -6 to 6
- sub_delays: int32 [4096, 1024], P('freq'), may hold values from 0 to 31, as said below
- merge_tables: int32 [4, 3, 4096], P(None, None, 'freq'), may hold values from 0 to 255, as said below
Outputs:
- peak_values: float32 [4, 8, 4096], P('beam', None, 'freq'), parts along dimension 0
The draws below stay inside these ranges and needn't reach their ends.
There are 2 independent parts, one for each index of `beam`. The reference program is written for one: setup_inputs(seed, part) draws one part's arguments, and reference() takes and returns one part's arrays. A program takes and returns all parts, laid end to end along the dimension named above; an argument that names none is the same for every part. Nothing has to cross between parts.
Inputs may be any that keep to these rules, and one draw needn't show every extreme that they name: `sub_delays`: every row has some channel with delay 32 - 1. `merge_tables`: for each level and each aligned block of 256 trials, rows 0 and 1 each hold a permutation of 0 to 255; row 2 holds delays of 0 to 63, and each such block has a delay of 63.
All inputs are finite; a program needn't handle non-finite values.
Results may differ from the reference program's by a relative error of at most 0.0003.
Values may be sent and summed in bfloat16 or wider, within the bound.
A program may use at most 128 MiB of HBM per device.

```python
import math
import jax
import jax.numpy as jnp
from jax import lax

COARSE = 1024
UPCHAN = 16
TAPS = 4
WIDTHS = 8
BEAMS = 2
NT = 256
DM_DEV = 256
SHIFTS = 32
LEVELS = 4
CROSS_SHIFT = 64
N_FREQ = 16


def draw_sub_delays(key, part):
    row_count = DM_DEV * N_FREQ
    col_count = COARSE * UPCHAN // N_FREQ
    first_key, second_key = jax.random.split(jax.random.fold_in(key, 11))
    base = jax.random.randint(first_key, (row_count, col_count), 0, SHIFTS)
    picked = jax.random.randint(second_key, (row_count, 1), 0, col_count)
    columns = jnp.arange(col_count)[None, :]
    return jnp.where(columns == picked, SHIFTS - 1, base).astype(jnp.int32)


def draw_merge_tables(key, part):
    blocks = LEVELS * N_FREQ
    keys = jax.random.split(jax.random.fold_in(key, 23), 2 * blocks + 2)
    permute = jax.vmap(lambda single: jax.random.permutation(single, DM_DEV))
    lower_rows = permute(keys[:blocks]).reshape(LEVELS, N_FREQ * DM_DEV)
    upper_rows = permute(keys[blocks:2 * blocks]).reshape(LEVELS, N_FREQ * DM_DEV)
    delays = jax.random.randint(keys[2 * blocks], (LEVELS, N_FREQ, DM_DEV), 0, CROSS_SHIFT)
    picked = jax.random.randint(keys[2 * blocks + 1], (LEVELS, N_FREQ, 1), 0, DM_DEV)
    delays = jnp.where(jnp.arange(DM_DEV)[None, None, :] == picked, CROSS_SHIFT - 1, delays)
    delays = delays.reshape(LEVELS, N_FREQ * DM_DEV)
    return jnp.stack([lower_rows, upper_rows, delays], axis=1).astype(jnp.int32)


def block_scale(stream_key, dims, pieces, smallest, largest):
    level, own = 1.0, jax.random.fold_in(stream_key, 6)
    for dim, blocks in pieces:
        heights = jnp.exp(jax.random.uniform(jax.random.fold_in(own, dim), (blocks,), jnp.float32, smallest / len(pieces), largest / len(pieces)))
        level = level * jnp.repeat(heights, dims[dim] // blocks).reshape([-1 if axis == dim else 1 for axis in range(len(dims))])
    return level


def noise(own_key, extent, scale, bound, cuts=(), kind=jnp.bfloat16):
    gain = block_scale(own_key, extent, cuts, -0.22, 0.18) if cuts else 1.0
    result = jax.random.normal(own_key, extent, jnp.float32) * scale * gain
    return jnp.minimum(jnp.maximum(result, -bound), bound).astype(kind)


def setup_inputs(seed: int = 0, part: int = 0) -> dict:
    arg_keys = jax.random.split(jax.random.key(seed), 4)
    part_splits = jax.random.split(jax.random.fold_in(arg_keys[3], part), 4)
    voltages = noise(part_splits[0], (2, BEAMS, COARSE, UPCHAN, NT), 1.0, 6.0, ((2, 16),))
    sub_delays = draw_sub_delays(jax.random.fold_in(arg_keys[3], 71), part)
    merge_tables = draw_merge_tables(jax.random.fold_in(arg_keys[3], 71), part)
    return {"voltages": voltages, "sub_delays": sub_delays, "merge_tables": merge_tables}


epsilon = 1e-06

def window_table(tap_count, upchan):
    length = tap_count * upchan
    positions = jnp.arange(length, dtype=jnp.float32)
    window = jnp.sinc((positions - (length - 1) / 2.0) / upchan)
    window = window * (0.5 - 0.5 * jnp.cos(2.0 * math.pi * (positions + 0.5) / length))
    window = window / jnp.sqrt(2.0 * jnp.sum(window * window))
    return window.reshape(tap_count, upchan)

def filter_power(volts):
    signal = volts.astype(jnp.float32)
    upchan = signal.shape[3]
    samples = signal.shape[4]
    window = window_table(TAPS, upchan)
    padded = jnp.pad(signal, ((0, 0), (0, 0), (0, 0), (0, 0), (TAPS - 1, 0)))
    filtered = jnp.zeros_like(signal)
    for offset in range(TAPS):
        filtered = filtered + window[offset][:, None] * padded[..., TAPS - 1 - offset:TAPS - 1 - offset + samples]
    phase = jnp.arange(upchan, dtype=jnp.float32)
    angle = 2.0 * math.pi * phase[:, None] * phase[None, :] / upchan
    cosine = jnp.cos(angle)
    sine_table = jnp.sin(angle)
    high = lax.Precision.HIGHEST
    real_part = jnp.einsum('km,bcmt->bckt', cosine, filtered[0], precision=high) + jnp.einsum('km,bcmt->bckt', sine_table, filtered[1], precision=high)
    imag_part = jnp.einsum('km,bcmt->bckt', cosine, filtered[1], precision=high) - jnp.einsum('km,bcmt->bckt', sine_table, filtered[0], precision=high)
    intensity = (real_part * real_part + imag_part * imag_part).astype(jnp.bfloat16)
    return intensity.reshape(signal.shape[1], signal.shape[2] * upchan, samples)

def shift_rows(series, delays):
    samples = series.shape[-1]
    source_time = jnp.arange(samples, dtype=jnp.int32) - delays[..., None]
    inside = source_time >= 0
    source_time = jnp.broadcast_to(jnp.maximum(source_time, 0), series.shape)
    picked = jnp.take_along_axis(series, source_time, axis=-1)
    return jnp.where(jnp.broadcast_to(inside, series.shape), picked, jnp.zeros_like(picked))

def boxcar_peaks(series):
    samples = series.shape[-1]
    row_mean = lax.optimization_barrier(jnp.mean(series, axis=-1, keepdims=True))
    centred = series - row_mean
    inv_scale = lax.rsqrt(lax.optimization_barrier(jnp.mean(centred * centred, axis=-1, keepdims=True)) + epsilon)
    boxcar = centred * inv_scale
    maxima = [lax.optimization_barrier(jnp.max(boxcar, axis=-1))]
    span_now = 1
    for offset in range(1, WIDTHS):
        lagged = jnp.pad(boxcar[..., :samples - span_now], ((0, 0), (0, 0), (span_now, 0)))
        boxcar = boxcar + lagged
        span_now = span_now * 2
        maxima.append(lax.optimization_barrier(jnp.max(boxcar, axis=-1)) / math.sqrt(span_now))
    return jnp.stack(maxima, axis=1)

def reference(voltages, sub_delays, merge_tables):
    coarse_dev = COARSE // N_FREQ
    natural = voltages.reshape(2, BEAMS, N_FREQ, coarse_dev, UPCHAN, NT)
    natural = natural.transpose(0, 1, 3, 2, 4, 5).reshape(2, BEAMS, COARSE, UPCHAN, NT)
    intensity = filter_power(natural)
    chan_dev = COARSE * UPCHAN // N_FREQ
    grouped = intensity.reshape(BEAMS, N_FREQ, chan_dev, NT).astype(jnp.float32)
    padded = jnp.pad(grouped, ((0, 0), (0, 0), (0, 0), (SHIFTS - 1, 0)))
    delay_table = sub_delays.reshape(N_FREQ, DM_DEV, chan_dev)

    def add_shift(running, shift_now):
        onehot = (delay_table == shift_now).astype(jnp.float32)
        start = (SHIFTS - 1 - shift_now).astype(jnp.int32)
        shifted_block = lax.dynamic_slice_in_dim(padded, start, NT, 3)
        return (running + jnp.einsum('grc,bgct->bgrt', onehot, shifted_block, precision=lax.Precision.HIGHEST), None)
    merged, _ = lax.scan(add_shift, jnp.zeros((BEAMS, N_FREQ, DM_DEV, NT), jnp.float32), jnp.arange(SHIFTS, dtype=jnp.int32))
    devices = jnp.arange(N_FREQ, dtype=jnp.int32)
    for merge_level in range(LEVELS):
        tables_now = merge_tables[merge_level].reshape(3, N_FREQ, DM_DEV)
        upper_bit = devices // 2 ** merge_level % 2
        lower_device = devices - upper_bit * 2 ** merge_level
        upper_device = lower_device + 2 ** merge_level
        lower_term = merged[:, lower_device[:, None], tables_now[0], :]
        upper_term = merged[:, upper_device[:, None], tables_now[1], :]
        merged = lower_term + shift_rows(upper_term, tables_now[2])
    return boxcar_peaks(merged.reshape(BEAMS, N_FREQ * DM_DEV, NT))
```

```python
import functools
import math

import jax
import jax.numpy as jnp
import ml_dtypes
import numpy as np
from jax import lax
from jax.experimental import pallas as pl
from jax.experimental.pallas import tpu as pltpu
from jax.sharding import PartitionSpec as P

TAPS = 4
WIDTHS = 8
SHIFTS = 32
CROSS_SHIFT = 64
PIECES = 3
VMEM_BYTES = 48 * 1024 * 1024
MESH = pl.DeviceIdType.MESH

epsilon = 1e-06


def filter_matrix(upchan):
    length = TAPS * upchan
    positions = np.arange(length, dtype=np.float64)
    window = np.sinc((positions - (length - 1) / 2.0) / upchan)
    window = window * (0.5 - 0.5 * np.cos(2.0 * math.pi * (positions + 0.5) / length))
    window = (window / np.sqrt(2.0 * np.sum(window * window))).reshape(TAPS, upchan)
    phase = np.arange(upchan)
    angle = 2.0 * math.pi * (phase[:, None] * phase[None, :] % upchan) / upchan
    cosine, sine = np.cos(angle), np.sin(angle)
    dft = np.stack([np.stack([cosine, sine], 1), np.stack([-sine, cosine], 1)], 0)
    full = dft[:, :, :, None, :] * window[None, None, None]
    full = full.reshape(2 * upchan, 2 * TAPS * upchan)
    pair = np.zeros((2, 2 * upchan, 2, 2 * TAPS * upchan))
    for channel in range(2):
        pair[channel, :, channel] = full
    pair = pair.reshape(4 * upchan, 4 * TAPS * upchan)
    rest, pieces = pair, []
    for _ in range(PIECES):
        piece = rest.astype(np.float32).astype(ml_dtypes.bfloat16)
        pieces.append(piece)
        rest = rest - piece.astype(np.float64)
    return np.concatenate(pieces, 0)


def filter_kernel(x_ref, w_ref, out_ref):
    _, beams, channels, upchan, samples = x_ref.shape
    width = beams * samples
    time = lax.broadcasted_iota(jnp.int32, (upchan, width), 1) % samples
    for first in range(0, channels, 2):
        tiles = []
        for channel in (first, first + 1):
            for part in range(2):
                signal = jnp.concatenate(
                    [x_ref[part, beam, channel] for beam in range(beams)], axis=1
                )
                tiles.append(signal)
                signal = signal.astype(jnp.float32)
                for tap in range(1, TAPS):
                    moved = jnp.where(time >= tap, pltpu.roll(signal, tap, 1), 0.0)
                    tiles.append(moved.astype(jnp.bfloat16))
        stacked = jnp.concatenate(tiles, axis=0)
        spectrum = jnp.dot(w_ref[...], stacked, preferred_element_type=jnp.float32)
        rows = 4 * upchan
        total = spectrum[2 * rows :] + spectrum[rows : 2 * rows]
        total = total + spectrum[:rows]
        for offset in range(2):
            real = total[2 * offset * upchan : (2 * offset + 1) * upchan]
            imag = total[(2 * offset + 1) * upchan : (2 * offset + 2) * upchan]
            start = (first + offset) * upchan
            out_ref[start : start + upchan, :] = (real * real + imag * imag).astype(jnp.bfloat16)


def filter_power(volts):
    _, beams, channels, upchan, samples = volts.shape
    block = min(8, channels)
    weights = jnp.asarray(filter_matrix(upchan))
    return pl.pallas_call(
        filter_kernel,
        grid=(channels // block,),
        in_specs=[
            pl.BlockSpec((2, beams, block, upchan, samples), lambda i: (0, 0, i, 0, 0)),
            pl.BlockSpec(weights.shape, lambda i: (0, 0)),
        ],
        out_specs=pl.BlockSpec((block * upchan, beams * samples), lambda i: (i, 0)),
        out_shape=jax.ShapeDtypeStruct((channels * upchan, beams * samples), jnp.bfloat16),
        compiler_params=pltpu.CompilerParams(vmem_limit_bytes=VMEM_BYTES),
        name="filterbank",
    )(volts, weights)


def dedisperse_kernel(sources, upchan, samples, x_ref, delay_ref, out_ref, ordered, total):
    channels, width = x_ref.shape
    each = channels // (sources * upchan)
    for source in range(sources):
        for index in range(each):
            start = (source * each + index) * upchan
            goal = (index * sources + source) * upchan
            ordered[goal : goal + upchan, :] = x_ref[start : start + upchan, :]
    total[...] = jnp.zeros_like(total)
    inside = lax.broadcasted_iota(jnp.int32, total.shape, 1) % samples >= 1

    def step(count, carry):
        shift = SHIFTS - 1 - count
        onehot = jnp.where(delay_ref[...] == shift, 1.0, 0.0).astype(jnp.bfloat16)
        term = jnp.dot(onehot, ordered[...], preferred_element_type=jnp.float32)
        total[...] = jnp.where(inside, pltpu.roll(total[...], 1, 1), 0.0) + term
        return carry

    lax.fori_loop(0, SHIFTS, step, 0)
    for beam in range(width // samples):
        out_ref[beam] = total[:, beam * samples : (beam + 1) * samples].T


def dedisperse(intensity, delays, sources, upchan, samples):
    rows = delays.shape[0]
    channels, width = intensity.shape
    return pl.pallas_call(
        functools.partial(dedisperse_kernel, sources, upchan, samples),
        out_shape=jax.ShapeDtypeStruct((width // samples, samples, rows), jnp.float32),
        in_specs=[pl.BlockSpec(memory_space=pltpu.VMEM)] * 2,
        out_specs=pl.BlockSpec(memory_space=pltpu.VMEM),
        scratch_shapes=[
            pltpu.VMEM((channels, width), jnp.bfloat16),
            pltpu.VMEM((rows, width), jnp.float32),
        ],
        compiler_params=pltpu.CompilerParams(vmem_limit_bytes=VMEM_BYTES),
        name="dedisperse",
    )(intensity, delays)


def later(series, amount):
    if amount % 8 == 0:
        zeros = jnp.zeros((amount, series.shape[1]), series.dtype)
        return jnp.concatenate([zeros, series[:-amount]], axis=0)
    time = lax.broadcasted_iota(jnp.int32, series.shape, 0)
    return jnp.where(time >= amount, pltpu.roll(series, amount, 0), 0.0)


def permuted(series, index):
    samples, rows = series.shape
    chosen = lax.broadcasted_iota(jnp.int32, (rows, index.shape[1]), 0) == index
    chosen = jnp.where(chosen, 1.0, 0.0).astype(jnp.bfloat16)
    rest, pieces = series, []
    for _ in range(PIECES):
        piece = rest.astype(jnp.bfloat16)
        pieces.append(piece)
        rest = rest - piece.astype(jnp.float32)
    moved = jnp.dot(
        jnp.concatenate(pieces, axis=0), chosen, preferred_element_type=jnp.float32
    )
    return (moved[:samples] + moved[samples : 2 * samples]) + moved[2 * samples :]


def merge_kernel(n, z_ref, table_ref, out_ref, pair, state, peaks, landed, sems, end_send, end_recv):
    levels = n.bit_length() - 1
    me = lax.axis_index("freq")
    half = n // 2
    barrier = pltpu.get_barrier_semaphore()
    partners = [me + (1 - 2 * (me // 2**level % 2)) * 2**level for level in range(levels)]
    goals = [slot * half + me // 2 for slot in range(2)]
    origins = [2 * (me % half) + beam for beam in range(2)]
    for partner in partners:
        pl.semaphore_signal(barrier, inc=1, device_id={"freq": partner}, device_id_type=MESH)
    for origin in origins:

        @pl.when(origin != me)
        def _():
            pl.semaphore_signal(barrier, inc=1, device_id={"freq": origin}, device_id_type=MESH)

    pl.semaphore_wait(barrier, levels + 1 + (me + n - 1) // n - (me + 1) // n)

    bit_count = max(CROSS_SHIFT - 1, 1).bit_length()
    final = None
    for level in range(levels):
        bit = me // 2**level % 2
        held = z_ref if level == 0 else state.at[level - 1]
        copy = pltpu.make_async_remote_copy(
            src_ref=held.at[1 - bit],
            dst_ref=pair.at[level, bit],
            send_sem=sems.at[0, level],
            recv_sem=sems.at[1, level],
            device_id={"freq": partners[level]},
            device_id_type=MESH,
        )
        copy.start()
        pair[level, bit] = held[bit]
        base = me // 2 ** (level + 1) * 2 ** (level + 1) + me // 2 % 2**level
        tables = [table_ref[base + slot * 2**level, level] for slot in range(2)]
        lower_index, upper_index, delays = (
            jnp.concatenate([table[row : row + 1] for table in tables], axis=1)
            for row in range(3)
        )
        copy.wait()
        upper = permuted(pair[level, 1], upper_index)
        for count in range(bit_count):
            upper = jnp.where((delays >> count) & 1 == 1, later(upper, 2**count), upper)
        merged = permuted(pair[level, 0], lower_index) + upper
        if level < levels - 1:
            rows = merged.shape[1] // 2
            state[level, 0] = merged[:, :rows]
            state[level, 1] = merged[:, rows:]
        else:
            final = merged

    samples, width = final.shape
    centred = final - jnp.mean(final, axis=0, keepdims=True)
    boxcar = centred * lax.rsqrt(jnp.mean(centred * centred, axis=0, keepdims=True) + epsilon)
    maxima = [jnp.max(boxcar, axis=0, keepdims=True)]
    for count in range(1, WIDTHS):
        boxcar = boxcar + later(boxcar, 2 ** (count - 1))
        maxima.append(jnp.max(boxcar, axis=0, keepdims=True) / math.sqrt(2**count))
    maxima = jnp.concatenate(maxima, axis=0)
    rows = width // 2
    beam = me % 2

    def send(slot):
        return pltpu.make_async_remote_copy(
            src_ref=peaks.at[slot],
            dst_ref=landed.at[beam],
            send_sem=end_send.at[slot],
            recv_sem=end_recv.at[beam],
            device_id={"freq": goals[slot]},
            device_id_type=MESH,
        )

    for slot in range(2):
        peaks[slot] = maxima[:, slot * rows : (slot + 1) * rows]
    for slot in range(2):

        @pl.when(goals[slot] != me)
        def _():
            send(slot).start()

        @pl.when(goals[slot] == me)
        def _():
            landed[beam] = peaks[slot]

    for slot in range(2):

        @pl.when(goals[slot] != me)
        def _():
            send(slot).wait_send()

    for source in range(2):

        @pl.when(origins[source] != me)
        def _():
            pltpu.make_async_remote_copy(
                src_ref=peaks.at[0],
                dst_ref=landed.at[source],
                send_sem=end_send.at[0],
                recv_sem=end_recv.at[source],
                device_id={"freq": origins[source]},
                device_id_type=MESH,
            ).wait_recv()

    out_ref[...] = landed[...]


def merge(series, tables, n):
    beams, samples, rows = series.shape
    levels = n.bit_length() - 1
    return pl.pallas_call(
        functools.partial(merge_kernel, n),
        out_shape=jax.ShapeDtypeStruct((beams, WIDTHS, rows), jnp.float32),
        in_specs=[pl.BlockSpec(memory_space=pltpu.VMEM)] * 2,
        out_specs=pl.BlockSpec(memory_space=pltpu.VMEM),
        scratch_shapes=[
            pltpu.VMEM((levels, 2, samples, rows), jnp.float32),
            pltpu.VMEM((levels - 1, 2, samples, rows), jnp.float32),
            pltpu.VMEM((2, WIDTHS, rows), jnp.float32),
            pltpu.VMEM((2, WIDTHS, rows), jnp.float32),
            pltpu.SemaphoreType.DMA((2, levels)),
            pltpu.SemaphoreType.DMA((2,)),
            pltpu.SemaphoreType.DMA((2,)),
        ],
        compiler_params=pltpu.CompilerParams(
            collective_id=1, has_side_effects=True, vmem_limit_bytes=VMEM_BYTES
        ),
        name="merge",
    )(series, tables)


def local(voltages, sub_delays, merge_tables):
    n = lax.axis_size("freq")
    upchan, samples = voltages.shape[3:]
    tables = lax.all_gather(merge_tables, "freq", axis=0)
    intensity = lax.all_to_all(
        filter_power(voltages), "freq", split_axis=0, concat_axis=0, tiled=True
    )
    series = dedisperse(intensity, sub_delays, n, upchan, samples)
    return merge(series, tables, n)


def solution(mesh):
    return jax.shard_map(
        local,
        mesh=mesh,
        in_specs=(P(None, "beam", "freq", None, None), P("freq", None), P(None, None, "freq")),
        out_specs=P("beam", None, "freq"),
        check_vma=False,
    )
```

```python
import functools
import math

import jax
import jax.numpy as jnp
import ml_dtypes
import numpy as np
from jax import lax
from jax.experimental import pallas as pl
from jax.experimental.pallas import tpu as pltpu
from jax.sharding import PartitionSpec as P

TAPS = 4
WIDTHS = 8
SHIFTS = 32
STRIDE = 4
CROSS_SHIFT = 64
PIECES = 3
VMEM_BYTES = 48 * 1024 * 1024
MESH = pl.DeviceIdType.MESH

epsilon = 1e-06


def filter_matrix(upchan, count):
    length = TAPS * upchan
    positions = np.arange(length, dtype=np.float64)
    window = np.sinc((positions - (length - 1) / 2.0) / upchan)
    window = window * (0.5 - 0.5 * np.cos(2.0 * math.pi * (positions + 0.5) / length))
    window = (window / np.sqrt(2.0 * np.sum(window * window))).reshape(TAPS, upchan)
    phase = np.arange(upchan)
    angle = 2.0 * math.pi * (phase[:, None] * phase[None, :] % upchan) / upchan
    cosine, sine = np.cos(angle), np.sin(angle)
    dft = np.stack([np.stack([cosine, sine], 1), np.stack([-sine, cosine], 1)], 0)
    full = dft[:, :, :, None, :] * window[None, None, None]
    full = full.reshape(2 * upchan, 2 * TAPS * upchan)
    pair = np.zeros((count, 2 * upchan, count, 2 * TAPS * upchan))
    for channel in range(count):
        pair[channel, :, channel] = full
    pair = pair.reshape(2 * count * upchan, 2 * count * TAPS * upchan)
    rest, pieces = pair, []
    for _ in range(PIECES):
        piece = rest.astype(np.float32).astype(ml_dtypes.bfloat16)
        pieces.append(piece)
        rest = rest - piece.astype(np.float64)
    return np.concatenate(pieces, 0)


def filter_chunk(x_ref, w_ref, first_channel, channels, write):
    _, beams, _, upchan, samples = x_ref.shape
    width = beams * samples
    count = w_ref.shape[1] // (2 * TAPS * upchan)
    time = lax.broadcasted_iota(jnp.int32, (upchan, width), 1) % samples
    for first in range(0, channels, count):
        tiles = []
        for channel in range(first, first + count):
            for part in range(2):
                signal = jnp.concatenate(
                    [x_ref[part, beam, first_channel + channel] for beam in range(beams)], axis=1
                )
                tiles.append(signal)
                signal = signal.astype(jnp.float32)
                for tap in range(1, TAPS):
                    moved = jnp.where(time >= tap, pltpu.roll(signal, tap, 1), 0.0)
                    tiles.append(moved.astype(jnp.bfloat16))
        stacked = jnp.concatenate(tiles, axis=0)
        spectrum = jnp.dot(w_ref[...], stacked, preferred_element_type=jnp.float32)
        rows = 2 * count * upchan
        total = spectrum[2 * rows :] + spectrum[rows : 2 * rows]
        total = total + spectrum[:rows]
        for offset in range(count):
            real = total[2 * offset * upchan : (2 * offset + 1) * upchan]
            imag = total[(2 * offset + 1) * upchan : (2 * offset + 2) * upchan]
            write(first + offset, (real * real + imag * imag).astype(jnp.bfloat16))


def exclusive_or(me, other, n):
    result = 0
    for bit in range(n.bit_length() - 1):
        result = result + (me // 2**bit % 2 + other // 2**bit % 2) % 2 * 2**bit
    return result


def table_places(me, level):
    size = 2**level
    base = me // (2 * size) * (2 * size)
    goals = [base + me % size * 2 + beam for beam in range(2)]
    origins = [base + me // 2 % size + slot * size for slot in range(2)]
    return goals, origins


def subband_kernel(
    n,
    x_ref,
    w_ref,
    delay_ref,
    table_ref,
    out_ref,
    tables_ref,
    outgoing,
    arrived,
    local_delays,
    shifted,
    total,
    part,
    tables,
    send_sem,
    recv_sem,
    table_send,
    table_recv,
):
    levels = n.bit_length() - 1
    me = lax.axis_index("freq")
    samples = x_ref.shape[4]
    _, each, upchan, width = arrived.shape
    rows, channels = delay_ref.shape
    groups, _, depth = local_delays.shape
    members = n // groups

    barrier = pltpu.get_barrier_semaphore()

    def greet(offset, carry):
        pl.semaphore_signal(
            barrier, inc=1, device_id={"freq": (me + offset) % n}, device_id_type=MESH
        )
        return carry

    lax.fori_loop(1, n, greet, 0)
    pl.semaphore_wait(barrier, n - 1)

    def table_copy(level, beam):
        goals, _ = table_places(me, level)
        slot = me // 2**level % 2
        return goals[beam], pltpu.make_async_remote_copy(
            src_ref=table_ref.at[level],
            dst_ref=tables.at[level, slot],
            send_sem=table_send.at[level, beam],
            recv_sem=table_recv.at[level, slot],
            device_id={"freq": goals[beam]},
            device_id_type=MESH,
        )

    def table_arrival(level, slot):
        _, origins = table_places(me, level)
        return origins[slot], pltpu.make_async_remote_copy(
            src_ref=table_ref.at[level],
            dst_ref=tables.at[level, slot],
            send_sem=table_send.at[level, 0],
            recv_sem=table_recv.at[level, slot],
            device_id={"freq": origins[slot]},
            device_id_type=MESH,
        )

    def chunk_copy(offset):
        return pltpu.make_async_remote_copy(
            src_ref=outgoing.at[offset],
            dst_ref=arrived.at[offset],
            send_sem=send_sem.at[offset],
            recv_sem=recv_sem.at[offset],
            device_id={"freq": exclusive_or(me, offset, n)},
            device_id_type=MESH,
        )

    def send_chunk(step, carry):
        offset = n - 1 - step

        def write(index, tile):
            outgoing[offset, index] = tile

        filter_chunk(x_ref, w_ref, exclusive_or(me, offset, n) * each, each, write)
        chunk_copy(offset).start()
        return carry

    lax.fori_loop(0, n - 1, send_chunk, 0)

    def write_own(index, tile):
        arrived[0, index] = tile

    filter_chunk(x_ref, w_ref, me * each, each, write_own)

    for level in range(levels):
        for beam in range(2):
            goal, copy = table_copy(level, beam)

            @pl.when(goal != me)
            def _():
                copy.start()

            @pl.when(goal == me)
            def _():
                tables[level, me // 2**level % 2] = table_ref[level]

    delays = delay_ref[...].astype(jnp.float32).astype(jnp.bfloat16)
    for group in range(groups):
        column = lax.broadcasted_iota(jnp.int32, (channels, depth), 1)
        index, fine = column // upchan % each, column % upchan
        source = me ^ (group * members + column // (each * upchan))
        wanted = index * (n * upchan) + source * upchan + fine
        chosen = lax.broadcasted_iota(jnp.int32, (channels, depth), 0) == wanted
        chosen = jnp.where(chosen, 1.0, 0.0).astype(jnp.bfloat16)
        local_delays[group] = jnp.dot(
            delays, chosen, preferred_element_type=jnp.float32
        ).astype(jnp.int32)

    time = lax.broadcasted_iota(jnp.int32, (depth, width), 1) % samples
    inside = lax.broadcasted_iota(jnp.int32, (rows, width), 1) % samples >= STRIDE
    for group in range(groups):
        for offset in range(group * members, (group + 1) * members):
            if offset > 0:
                chunk_copy(offset).wait_recv()
        block = arrived[group * members : (group + 1) * members].reshape(depth, width)
        shifted[:depth] = block
        block = block.astype(jnp.float32)
        for shift in range(1, STRIDE):
            moved = jnp.where(time >= shift, pltpu.roll(block, shift, 1), 0.0)
            shifted[shift * depth : (shift + 1) * depth] = moved.astype(jnp.bfloat16)
        part[...] = jnp.zeros_like(part)

        def horner(step, carry):
            base = SHIFTS - STRIDE - STRIDE * step
            group_delays = local_delays[group]
            onehot = jnp.concatenate(
                [
                    jnp.where(group_delays == base + shift, 1.0, 0.0).astype(jnp.bfloat16)
                    for shift in range(STRIDE)
                ],
                axis=1,
            )
            term = jnp.dot(onehot, shifted[...], preferred_element_type=jnp.float32)
            part[...] = jnp.where(inside, pltpu.roll(part[...], STRIDE, 1), 0.0) + term
            return carry

        lax.fori_loop(0, SHIFTS // STRIDE, horner, 0)
        if group == 0:
            total[...] = part[...]
        elif group < groups - 1:
            total[...] += part[...]
    summed = total[...] + part[...] if groups > 1 else part[...]
    for beam in range(width // samples):
        out_ref[beam] = summed[:, beam * samples : (beam + 1) * samples].T

    for level in range(levels):
        for slot in range(2):
            origin, arrival = table_arrival(level, slot)

            @pl.when(origin != me)
            def _():
                arrival.wait_recv()

        for beam in range(2):
            goal, copy = table_copy(level, beam)

            @pl.when(goal != me)
            def _():
                copy.wait_send()

    tables_ref[...] = tables[...]

    def sent(offset, carry):
        chunk_copy(offset).wait_send()
        return carry

    lax.fori_loop(1, n, sent, 0)


def subbands(volts, delays, merge_tables, n):
    _, beams, coarse, upchan, samples = volts.shape
    rows, channels = delays.shape
    levels = n.bit_length() - 1
    each = coarse // n
    width = beams * samples
    members = max(1, min(n, 256 // (each * upchan)))
    depth = members * each * upchan
    weights = jnp.asarray(filter_matrix(upchan, 2 if each % 2 == 0 else 1))
    vmem = pl.BlockSpec(memory_space=pltpu.VMEM)
    return pl.pallas_call(
        functools.partial(subband_kernel, n),
        out_shape=(
            jax.ShapeDtypeStruct((beams, samples, rows), jnp.float32),
            jax.ShapeDtypeStruct((levels, 2, 3, rows), jnp.int32),
        ),
        in_specs=[vmem] * 4,
        out_specs=(vmem, vmem),
        scratch_shapes=[
            pltpu.VMEM((n, each, upchan, width), jnp.bfloat16),
            pltpu.VMEM((n, each, upchan, width), jnp.bfloat16),
            pltpu.VMEM((n // members, rows, depth), jnp.int32),
            pltpu.VMEM((STRIDE * depth, width), jnp.bfloat16),
            pltpu.VMEM((rows, width), jnp.float32),
            pltpu.VMEM((rows, width), jnp.float32),
            pltpu.VMEM((levels, 2, 3, rows), jnp.int32),
            pltpu.SemaphoreType.DMA((n,)),
            pltpu.SemaphoreType.DMA((n,)),
            pltpu.SemaphoreType.DMA((levels, 2)),
            pltpu.SemaphoreType.DMA((levels, 2)),
        ],
        compiler_params=pltpu.CompilerParams(
            collective_id=0, has_side_effects=True, vmem_limit_bytes=VMEM_BYTES
        ),
        name="subbands",
    )(volts, weights, delays, merge_tables)


def later(series, amount):
    if amount % 8 == 0:
        zeros = jnp.zeros((amount, series.shape[1]), series.dtype)
        return jnp.concatenate([zeros, series[:-amount]], axis=0)
    time = lax.broadcasted_iota(jnp.int32, series.shape, 0)
    return jnp.where(time >= amount, pltpu.roll(series, amount, 0), 0.0)


def permuted(series, index):
    samples, rows = series.shape
    chosen = lax.broadcasted_iota(jnp.int32, (rows, index.shape[1]), 0) == index
    chosen = jnp.where(chosen, 1.0, 0.0).astype(jnp.bfloat16)
    rest, pieces = series, []
    for _ in range(PIECES):
        piece = rest.astype(jnp.bfloat16)
        pieces.append(piece)
        rest = rest - piece.astype(jnp.float32)
    moved = jnp.dot(
        jnp.concatenate(pieces, axis=0), chosen, preferred_element_type=jnp.float32
    )
    return (moved[:samples] + moved[samples : 2 * samples]) + moved[2 * samples :]


def merge_kernel(n, z_ref, table_ref, out_ref, pair, state, peaks, landed, sems, end_send, end_recv):
    levels = n.bit_length() - 1
    me = lax.axis_index("freq")
    half = n // 2
    barrier = pltpu.get_barrier_semaphore()
    partners = [me + (1 - 2 * (me // 2**level % 2)) * 2**level for level in range(levels)]
    goals = [slot * half + me // 2 for slot in range(2)]
    origins = [2 * (me % half) + beam for beam in range(2)]
    for partner in partners:
        pl.semaphore_signal(barrier, inc=1, device_id={"freq": partner}, device_id_type=MESH)
    for origin in origins:

        @pl.when(origin != me)
        def _():
            pl.semaphore_signal(barrier, inc=1, device_id={"freq": origin}, device_id_type=MESH)

    pl.semaphore_wait(barrier, levels + 1 + (me + n - 1) // n - (me + 1) // n)

    bit_count = max(CROSS_SHIFT - 1, 1).bit_length()
    final = None
    for level in range(levels):
        bit = me // 2**level % 2
        held = z_ref if level == 0 else state.at[level - 1]
        copy = pltpu.make_async_remote_copy(
            src_ref=held.at[1 - bit],
            dst_ref=pair.at[level, bit],
            send_sem=sems.at[0, level],
            recv_sem=sems.at[1, level],
            device_id={"freq": partners[level]},
            device_id_type=MESH,
        )
        copy.start()
        pair[level, bit] = held[bit]
        tables = [table_ref[level, slot] for slot in range(2)]
        lower_index, upper_index, delays = (
            jnp.concatenate([table[row : row + 1] for table in tables], axis=1)
            for row in range(3)
        )
        copy.wait()
        upper = permuted(pair[level, 1], upper_index)
        for count in range(bit_count):
            upper = jnp.where((delays >> count) & 1 == 1, later(upper, 2**count), upper)
        merged = permuted(pair[level, 0], lower_index) + upper
        if level < levels - 1:
            rows = merged.shape[1] // 2
            state[level, 0] = merged[:, :rows]
            state[level, 1] = merged[:, rows:]
        else:
            final = merged

    samples, width = final.shape
    centred = final - jnp.mean(final, axis=0, keepdims=True)
    boxcar = centred * lax.rsqrt(jnp.mean(centred * centred, axis=0, keepdims=True) + epsilon)
    maxima = [jnp.max(boxcar, axis=0, keepdims=True)]
    for count in range(1, WIDTHS):
        boxcar = boxcar + later(boxcar, 2 ** (count - 1))
        maxima.append(jnp.max(boxcar, axis=0, keepdims=True) / math.sqrt(2**count))
    maxima = jnp.concatenate(maxima, axis=0)
    rows = width // 2
    beam = me % 2

    def send(slot):
        return pltpu.make_async_remote_copy(
            src_ref=peaks.at[slot],
            dst_ref=landed.at[beam],
            send_sem=end_send.at[slot],
            recv_sem=end_recv.at[beam],
            device_id={"freq": goals[slot]},
            device_id_type=MESH,
        )

    for slot in range(2):
        peaks[slot] = maxima[:, slot * rows : (slot + 1) * rows]
    for slot in range(2):

        @pl.when(goals[slot] != me)
        def _():
            send(slot).start()

        @pl.when(goals[slot] == me)
        def _():
            landed[beam] = peaks[slot]

    for slot in range(2):

        @pl.when(goals[slot] != me)
        def _():
            send(slot).wait_send()

    for source in range(2):

        @pl.when(origins[source] != me)
        def _():
            pltpu.make_async_remote_copy(
                src_ref=peaks.at[0],
                dst_ref=landed.at[source],
                send_sem=end_send.at[0],
                recv_sem=end_recv.at[source],
                device_id={"freq": origins[source]},
                device_id_type=MESH,
            ).wait_recv()

    out_ref[...] = landed[...]


def merge(series, tables, n):
    beams, samples, rows = series.shape
    levels = n.bit_length() - 1
    return pl.pallas_call(
        functools.partial(merge_kernel, n),
        out_shape=jax.ShapeDtypeStruct((beams, WIDTHS, rows), jnp.float32),
        in_specs=[pl.BlockSpec(memory_space=pltpu.VMEM)] * 2,
        out_specs=pl.BlockSpec(memory_space=pltpu.VMEM),
        scratch_shapes=[
            pltpu.VMEM((levels, 2, samples, rows), jnp.float32),
            pltpu.VMEM((levels - 1, 2, samples, rows), jnp.float32),
            pltpu.VMEM((2, WIDTHS, rows), jnp.float32),
            pltpu.VMEM((2, WIDTHS, rows), jnp.float32),
            pltpu.SemaphoreType.DMA((2, levels)),
            pltpu.SemaphoreType.DMA((2,)),
            pltpu.SemaphoreType.DMA((2,)),
        ],
        compiler_params=pltpu.CompilerParams(
            collective_id=1, has_side_effects=True, vmem_limit_bytes=VMEM_BYTES
        ),
        name="merge",
    )(series, tables)


def local(voltages, sub_delays, merge_tables):
    n = lax.axis_size("freq")
    series, tables = subbands(voltages, sub_delays, merge_tables, n)
    return merge(series, tables, n)


def solution(mesh):
    return jax.shard_map(
        local,
        mesh=mesh,
        in_specs=(P(None, "beam", "freq", None, None), P("freq", None), P(None, None, "freq")),
        out_specs=P("beam", None, "freq"),
        check_vma=False,
    )
```

```python
import functools
import math

import jax
import jax.numpy as jnp
import ml_dtypes
import numpy as np
from jax import lax
from jax.experimental import pallas as pl
from jax.experimental.pallas import tpu as pltpu
from jax.sharding import PartitionSpec as P

TAPS = 4
WIDTHS = 8
SHIFTS = 32
STRIDE = 4
CROSS_SHIFT = 64
PIECES = 3
VMEM_BYTES = 48 * 1024 * 1024
SUBBAND_BYTES = 63 * 1024 * 1024
MESH = pl.DeviceIdType.MESH

epsilon = 1e-06


def filter_matrix(upchan, count):
    length = TAPS * upchan
    positions = np.arange(length, dtype=np.float64)
    window = np.sinc((positions - (length - 1) / 2.0) / upchan)
    window = window * (0.5 - 0.5 * np.cos(2.0 * math.pi * (positions + 0.5) / length))
    window = (window / np.sqrt(2.0 * np.sum(window * window))).reshape(TAPS, upchan)
    phase = np.arange(upchan)
    angle = 2.0 * math.pi * (phase[:, None] * phase[None, :] % upchan) / upchan
    cosine, sine = np.cos(angle), np.sin(angle)
    dft = np.stack([np.stack([cosine, sine], 1), np.stack([-sine, cosine], 1)], 0)
    full = dft[:, :, :, None, :] * window[None, None, None]
    full = full.reshape(2 * upchan, 2 * TAPS * upchan)
    pair = np.zeros((count, 2 * upchan, count, 2 * TAPS * upchan))
    for channel in range(count):
        pair[channel, :, channel] = full
    pair = pair.reshape(2 * count * upchan, 2 * count * TAPS * upchan)
    rest, pieces = pair, []
    for _ in range(PIECES):
        piece = rest.astype(np.float32).astype(ml_dtypes.bfloat16)
        pieces.append(piece)
        rest = rest - piece.astype(np.float64)
    return np.concatenate(pieces, 0)


def filter_chunk(x_ref, w_ref, first_channel, channels, write):
    _, beams, _, upchan, samples = x_ref.shape
    width = beams * samples
    count = w_ref.shape[1] // (2 * TAPS * upchan)
    time = lax.broadcasted_iota(jnp.int32, (upchan, width), 1) % samples
    for first in range(0, channels, count):
        tiles = []
        for channel in range(first, first + count):
            for part in range(2):
                signal = jnp.concatenate(
                    [x_ref[part, beam, first_channel + channel] for beam in range(beams)], axis=1
                )
                tiles.append(signal)
                signal = signal.astype(jnp.float32)
                for tap in range(1, TAPS):
                    moved = jnp.where(time >= tap, pltpu.roll(signal, tap, 1), 0.0)
                    tiles.append(moved.astype(jnp.bfloat16))
        stacked = jnp.concatenate(tiles, axis=0)
        spectrum = jnp.dot(w_ref[...], stacked, preferred_element_type=jnp.float32)
        rows = 2 * count * upchan
        total = spectrum[2 * rows :] + spectrum[rows : 2 * rows]
        total = total + spectrum[:rows]
        for offset in range(count):
            real = total[2 * offset * upchan : (2 * offset + 1) * upchan]
            imag = total[(2 * offset + 1) * upchan : (2 * offset + 2) * upchan]
            write(first + offset, (real * real + imag * imag).astype(jnp.bfloat16))


def exclusive_or(me, other, n):
    result = 0
    for bit in range(n.bit_length() - 1):
        result = result + (me // 2**bit % 2 + other // 2**bit % 2) % 2 * 2**bit
    return result


def table_places(me, level):
    size = 2**level
    base = me // (2 * size) * (2 * size)
    goals = [base + me % size * 2 + beam for beam in range(2)]
    origins = [base + me // 2 % size + slot * size for slot in range(2)]
    return goals, origins


def subband_kernel(
    n,
    x_hbm,
    w_hbm,
    delay_hbm,
    table_hbm,
    out_ref,
    tables_ref,
    x_ref,
    w_ref,
    delay_ref,
    table_ref,
    weights,
    level_tables,
    outgoing,
    arrived,
    local_delays,
    shifted,
    total,
    part,
    tables,
    send_sem,
    recv_sem,
    table_send,
    table_recv,
    input_sem,
):
    levels = n.bit_length() - 1
    me = lax.axis_index("freq")
    samples = x_ref.shape[4]
    _, each, upchan, width = arrived.shape
    rows, channels = delay_ref.shape
    groups, _, depth = local_delays.shape
    members = n // groups

    inputs = [
        pltpu.make_async_copy(source, goal, input_sem.at[place])
        for place, (source, goal) in enumerate(
            [(x_hbm, x_ref), (w_hbm, w_ref), (delay_hbm, delay_ref), (table_hbm, table_ref)]
        )
    ]
    for copy in inputs:
        copy.start()

    barrier = pltpu.get_barrier_semaphore()

    def greet(offset, carry):
        pl.semaphore_signal(
            barrier, inc=1, device_id={"freq": (me + offset) % n}, device_id_type=MESH
        )
        return carry

    lax.fori_loop(1, n, greet, 0)
    pl.semaphore_wait(barrier, n - 1)
    inputs[0].wait()
    inputs[1].wait()
    weights[...] = w_ref[...].astype(jnp.bfloat16)

    def table_copy(level, beam):
        goals, _ = table_places(me, level)
        slot = me // 2**level % 2
        return goals[beam], pltpu.make_async_remote_copy(
            src_ref=level_tables.at[level],
            dst_ref=tables.at[level, slot],
            send_sem=table_send.at[level, beam],
            recv_sem=table_recv.at[level, slot],
            device_id={"freq": goals[beam]},
            device_id_type=MESH,
        )

    def table_arrival(level, slot):
        _, origins = table_places(me, level)
        return origins[slot], pltpu.make_async_remote_copy(
            src_ref=level_tables.at[level],
            dst_ref=tables.at[level, slot],
            send_sem=table_send.at[level, 0],
            recv_sem=table_recv.at[level, slot],
            device_id={"freq": origins[slot]},
            device_id_type=MESH,
        )

    def chunk_copy(offset):
        return pltpu.make_async_remote_copy(
            src_ref=outgoing.at[offset],
            dst_ref=arrived.at[offset],
            send_sem=send_sem.at[offset],
            recv_sem=recv_sem.at[offset],
            device_id={"freq": exclusive_or(me, offset, n)},
            device_id_type=MESH,
        )

    def send_chunk(offset, carry):

        def write(index, tile):
            outgoing[offset, index] = tile

        filter_chunk(x_ref, weights, exclusive_or(me, offset, n) * each, each, write)
        chunk_copy(offset).start()
        return carry

    half = n // 2
    early = min(half + members, n)
    lax.fori_loop(half, early, send_chunk, 0)
    lax.fori_loop(1, half, send_chunk, 0)

    def write_own(index, tile):
        arrived[0, index] = tile

    filter_chunk(x_ref, weights, me * each, each, write_own)
    lax.fori_loop(early, n, send_chunk, 0)
    inputs[2].wait()
    inputs[3].wait()
    for level in range(levels):
        for row in range(3):
            level_tables[level, row : row + 1] = table_ref[row, level : level + 1]

    for level in range(levels):
        for beam in range(2):
            goal, copy = table_copy(level, beam)

            @pl.when(goal != me)
            def _():
                copy.start()

            @pl.when(goal == me)
            def _():
                tables[level, me // 2**level % 2] = level_tables[level]

    delays = delay_ref[...].astype(jnp.float32).astype(jnp.bfloat16)
    for group in range(groups):
        column = lax.broadcasted_iota(jnp.int32, (1, depth), 1)
        index, fine = column // upchan % each, column % upchan
        source = me ^ (group * members + column // (each * upchan))
        wanted = index * (n * upchan) + source * upchan + fine
        chosen = lax.broadcasted_iota(jnp.int32, (channels, depth), 0) == wanted
        chosen = jnp.where(chosen, 1.0, 0.0).astype(jnp.bfloat16)
        local_delays[group] = jnp.dot(
            delays, chosen, preferred_element_type=jnp.float32
        ).astype(jnp.int32)

    time = lax.broadcasted_iota(jnp.int32, (depth, width), 1) % samples
    inside = lax.broadcasted_iota(jnp.int32, (rows, width), 1) % samples >= STRIDE
    for group in range(groups):
        for offset in range(group * members, (group + 1) * members):
            if offset > 0:
                chunk_copy(offset).wait_recv()
        block = arrived[group * members : (group + 1) * members].reshape(depth, width)
        shifted[:depth] = block
        block = block.astype(jnp.float32)
        for shift in range(1, STRIDE):
            moved = jnp.where(time >= shift, pltpu.roll(block, shift, 1), 0.0)
            shifted[shift * depth : (shift + 1) * depth] = moved.astype(jnp.bfloat16)
        part[...] = jnp.zeros_like(part)

        def horner(step, carry):
            base = SHIFTS - STRIDE - STRIDE * step
            group_delays = local_delays[group]
            onehot = jnp.concatenate(
                [
                    jnp.where(group_delays == base + shift, 1.0, 0.0).astype(jnp.bfloat16)
                    for shift in range(STRIDE)
                ],
                axis=1,
            )
            term = jnp.dot(onehot, shifted[...], preferred_element_type=jnp.float32)
            part[...] = jnp.where(inside, pltpu.roll(part[...], STRIDE, 1), 0.0) + term
            return carry

        lax.fori_loop(0, SHIFTS // STRIDE, horner, 0)
        if group == 0:
            total[...] = part[...]
        elif group < groups - 1:
            total[...] += part[...]
    summed = total[...] + part[...] if groups > 1 else part[...]
    for beam in range(width // samples):
        out_ref[beam] = summed[:, beam * samples : (beam + 1) * samples].T

    for level in range(levels):
        for slot in range(2):
            origin, arrival = table_arrival(level, slot)

            @pl.when(origin != me)
            def _():
                arrival.wait_recv()

        for beam in range(2):
            goal, copy = table_copy(level, beam)

            @pl.when(goal != me)
            def _():
                copy.wait_send()

    tables_ref[...] = tables[...]

    def sent(offset, carry):
        chunk_copy(offset).wait_send()
        return carry

    lax.fori_loop(1, n, sent, 0)


def subbands(volts, delays, merge_tables, n):
    _, beams, coarse, upchan, samples = volts.shape
    rows, channels = delays.shape
    levels = n.bit_length() - 1
    each = coarse // n
    width = beams * samples
    members = max(1, min(n, 256 // (each * upchan)))
    depth = members * each * upchan
    weights = jnp.asarray(filter_matrix(upchan, 2 if each % 2 == 0 else 1).astype(np.float32))
    merge_tables = merge_tables.transpose(1, 0, 2)
    vmem = pl.BlockSpec(memory_space=pltpu.VMEM)
    return pl.pallas_call(
        functools.partial(subband_kernel, n),
        out_shape=(
            jax.ShapeDtypeStruct((beams, samples, rows), jnp.float32),
            jax.ShapeDtypeStruct((levels, 2, 3, rows), jnp.int32),
        ),
        in_specs=[pl.BlockSpec(memory_space=pltpu.HBM)] * 4,
        out_specs=(vmem, vmem),
        scratch_shapes=[
            pltpu.VMEM(volts.shape, volts.dtype),
            pltpu.VMEM(weights.shape, weights.dtype),
            pltpu.VMEM(delays.shape, delays.dtype),
            pltpu.VMEM(merge_tables.shape, merge_tables.dtype),
            pltpu.VMEM(weights.shape, jnp.bfloat16),
            pltpu.VMEM((levels, 3, rows), jnp.int32),
            pltpu.VMEM((n, each, upchan, width), jnp.bfloat16),
            pltpu.VMEM((n, each, upchan, width), jnp.bfloat16),
            pltpu.VMEM((n // members, rows, depth), jnp.int32),
            pltpu.VMEM((STRIDE * depth, width), jnp.bfloat16),
            pltpu.VMEM((rows, width), jnp.float32),
            pltpu.VMEM((rows, width), jnp.float32),
            pltpu.VMEM((levels, 2, 3, rows), jnp.int32),
            pltpu.SemaphoreType.DMA((n,)),
            pltpu.SemaphoreType.DMA((n,)),
            pltpu.SemaphoreType.DMA((levels, 2)),
            pltpu.SemaphoreType.DMA((levels, 2)),
            pltpu.SemaphoreType.DMA((4,)),
        ],
        compiler_params=pltpu.CompilerParams(
            collective_id=0, has_side_effects=True, vmem_limit_bytes=SUBBAND_BYTES
        ),
        name="subbands",
    )(volts, weights, delays, merge_tables)


def later(series, amount):
    if amount % 8 == 0:
        zeros = jnp.zeros((amount, series.shape[1]), series.dtype)
        return jnp.concatenate([zeros, series[:-amount]], axis=0)
    time = lax.broadcasted_iota(jnp.int32, series.shape, 0)
    return jnp.where(time >= amount, pltpu.roll(series, amount, 0), 0.0)


def delayed(before, series, delays):
    count = series.shape[0]
    current = jnp.concatenate([before, series], axis=0)
    for bit in reversed(range(max(CROSS_SHIFT - 1, 1).bit_length())):
        amount = 2**bit
        chosen = (delays >> bit) & 1 == 1
        if amount >= 8:
            height = count + -(-(amount - 1) // 8) * 8
            first = current.shape[0] - height
            moved = current[first - amount : first - amount + height]
            current = jnp.where(chosen, moved, current[first:])
        else:
            current = jnp.where(chosen, pltpu.roll(current, amount, 0), current)
    return current[current.shape[0] - count :]


def permuted(series, chosen):
    samples = series.shape[0]
    rest, pieces = series, []
    for _ in range(PIECES):
        piece = rest.astype(jnp.bfloat16)
        pieces.append(piece)
        rest = rest - piece.astype(jnp.float32)
    moved = jnp.dot(
        jnp.concatenate(pieces, axis=0), chosen, preferred_element_type=jnp.float32
    )
    return (moved[:samples] + moved[samples : 2 * samples]) + moved[2 * samples :]


def merge_kernel(
    n, z_ref, table_ref, out_ref, taken, state, chosen, previous, final, peaks, landed, sems, end_send, end_recv
):
    levels = n.bit_length() - 1
    me = lax.axis_index("freq")
    half = n // 2
    barrier = pltpu.get_barrier_semaphore()
    partners = [me + (1 - 2 * (me // 2**level % 2)) * 2**level for level in range(levels)]
    goals = [slot * half + me // 2 for slot in range(2)]
    origins = [2 * (me % half) + beam for beam in range(2)]
    for partner in partners:
        pl.semaphore_signal(barrier, inc=1, device_id={"freq": partner}, device_id_type=MESH)
    for origin in origins:

        @pl.when(origin != me)
        def _():
            pl.semaphore_signal(barrier, inc=1, device_id={"freq": origin}, device_id_type=MESH)

    pl.semaphore_wait(barrier, levels + 1 + (me + n - 1) // n - (me + 1) // n)

    samples, width = final.shape
    rows = width // 2
    piece = min(CROSS_SHIFT, samples)
    chunks = samples // piece

    def exchange(level, chunk):
        held = z_ref if level == 0 else state.at[level - 1]
        span = pl.ds(chunk * piece, piece)
        return pltpu.make_async_remote_copy(
            src_ref=held.at[1 - me // 2**level % 2, span],
            dst_ref=taken.at[level, span],
            send_sem=sems.at[0, level, chunk],
            recv_sem=sems.at[1, level, chunk],
            device_id={"freq": partners[level]},
            device_id_type=MESH,
        )

    def columns(level, row):
        return jnp.concatenate([table_ref[level, slot, row : row + 1] for slot in range(2)], axis=1)

    for chunk in range(chunks):
        exchange(0, chunk).start()
    for level in range(levels):
        for row in range(2):
            onehot = lax.broadcasted_iota(jnp.int32, (rows, width), 0) == columns(level, row)
            chosen[level, row] = jnp.where(onehot, 1.0, 0.0).astype(jnp.bfloat16)
    for diagonal in range(levels + chunks - 1):
        for level in reversed(range(levels)):
            chunk = diagonal - level
            if not 0 <= chunk < chunks:
                continue
            span = slice(chunk * piece, (chunk + 1) * piece)
            bit = me // 2**level % 2
            kept = z_ref[bit, span] if level == 0 else state[level - 1, bit, span]
            exchange(level, chunk).wait_recv()
            other = taken[level, span]
            lower = jnp.where(bit == 0, kept, other)
            upper = jnp.where(bit == 0, other, kept)
            upper = permuted(upper, chosen[level, 1])
            before = jnp.zeros_like(upper) if chunk == 0 else previous[level]
            if chunk < chunks - 1:
                previous[level] = upper
            merged = permuted(lower, chosen[level, 0]) + delayed(before, upper, columns(level, 2))
            if level < levels - 1:
                state[level, 0, span] = merged[:, :rows]
                state[level, 1, span] = merged[:, rows:]
                exchange(level + 1, chunk).start()
            else:
                final[span] = merged

    final = final[...]
    centred = final - jnp.mean(final, axis=0, keepdims=True)
    boxcar = centred * lax.rsqrt(jnp.mean(centred * centred, axis=0, keepdims=True) + epsilon)
    maxima = [jnp.max(boxcar, axis=0, keepdims=True)]
    for count in range(1, WIDTHS):
        boxcar = boxcar + later(boxcar, 2 ** (count - 1))
        maxima.append(jnp.max(boxcar, axis=0, keepdims=True) / math.sqrt(2**count))
    maxima = jnp.concatenate(maxima, axis=0)
    beam = me % 2

    def send(slot):
        return pltpu.make_async_remote_copy(
            src_ref=peaks.at[slot],
            dst_ref=landed.at[beam],
            send_sem=end_send.at[slot],
            recv_sem=end_recv.at[beam],
            device_id={"freq": goals[slot]},
            device_id_type=MESH,
        )

    for slot in range(2):
        peaks[slot] = maxima[:, slot * rows : (slot + 1) * rows]
    for slot in range(2):

        @pl.when(goals[slot] != me)
        def _():
            send(slot).start()

        @pl.when(goals[slot] == me)
        def _():
            landed[beam] = peaks[slot]

    for slot in range(2):

        @pl.when(goals[slot] != me)
        def _():
            send(slot).wait_send()

    for source in range(2):

        @pl.when(origins[source] != me)
        def _():
            pltpu.make_async_remote_copy(
                src_ref=peaks.at[0],
                dst_ref=landed.at[source],
                send_sem=end_send.at[0],
                recv_sem=end_recv.at[source],
                device_id={"freq": origins[source]},
                device_id_type=MESH,
            ).wait_recv()

    out_ref[...] = landed[...]
    for level in range(levels):
        for chunk in range(chunks):
            exchange(level, chunk).wait_send()


def merge(series, tables, n):
    beams, samples, rows = series.shape
    levels = n.bit_length() - 1
    return pl.pallas_call(
        functools.partial(merge_kernel, n),
        out_shape=jax.ShapeDtypeStruct((beams, WIDTHS, rows), jnp.float32),
        in_specs=[pl.BlockSpec(memory_space=pltpu.VMEM)] * 2,
        out_specs=pl.BlockSpec(memory_space=pltpu.VMEM),
        scratch_shapes=[
            pltpu.VMEM((levels, samples, rows), jnp.float32),
            pltpu.VMEM((levels - 1, 2, samples, rows), jnp.float32),
            pltpu.VMEM((levels, 2, rows, 2 * rows), jnp.bfloat16),
            pltpu.VMEM((levels, min(CROSS_SHIFT, samples), 2 * rows), jnp.float32),
            pltpu.VMEM((samples, 2 * rows), jnp.float32),
            pltpu.VMEM((2, WIDTHS, rows), jnp.float32),
            pltpu.VMEM((2, WIDTHS, rows), jnp.float32),
            pltpu.SemaphoreType.DMA((2, levels, samples // min(CROSS_SHIFT, samples))),
            pltpu.SemaphoreType.DMA((2,)),
            pltpu.SemaphoreType.DMA((2,)),
        ],
        compiler_params=pltpu.CompilerParams(
            collective_id=1, has_side_effects=True, vmem_limit_bytes=VMEM_BYTES
        ),
        name="merge",
    )(series, tables)


def local(voltages, sub_delays, merge_tables):
    n = lax.axis_size("freq")
    series, tables = subbands(voltages, sub_delays, merge_tables, n)
    return merge(series, tables, n)


def solution(mesh):
    return jax.shard_map(
        local,
        mesh=mesh,
        in_specs=(P(None, "beam", "freq", None, None), P("freq", None), P(None, None, "freq")),
        out_specs=P("beam", None, "freq"),
        check_vma=False,
    )
```

```python
import functools
import math

import jax
import jax.numpy as jnp
import ml_dtypes
import numpy as np
from jax import lax
from jax.experimental import pallas as pl
from jax.experimental.pallas import tpu as pltpu
from jax.sharding import PartitionSpec as P

TAPS = 4
WIDTHS = 8
SHIFTS = 32
LANES = 128
STRIDE = 4
CROSS_SHIFT = 64
PIECES = 3
VMEM_BYTES = 63 * 1024 * 1024
MESH = pl.DeviceIdType.MESH

epsilon = 1e-06


def filter_matrix(upchan, count):
    length = TAPS * upchan
    positions = np.arange(length, dtype=np.float64)
    window = np.sinc((positions - (length - 1) / 2.0) / upchan)
    window = window * (0.5 - 0.5 * np.cos(2.0 * math.pi * (positions + 0.5) / length))
    window = (window / np.sqrt(2.0 * np.sum(window * window))).reshape(TAPS, upchan)
    phase = np.arange(upchan)
    angle = 2.0 * math.pi * (phase[:, None] * phase[None, :] % upchan) / upchan
    cosine, sine = np.cos(angle), np.sin(angle)
    dft = np.stack([np.stack([cosine, sine], 1), np.stack([-sine, cosine], 1)], 0)
    full = dft[:, :, :, None, :] * window[None, None, None]
    full = full.reshape(2 * upchan, 2 * TAPS * upchan)
    pair = np.zeros((count, 2 * upchan, count, 2 * TAPS * upchan))
    for channel in range(count):
        pair[channel, :, channel] = full
    pair = pair.reshape(2 * count * upchan, 2 * count * TAPS * upchan)
    rest, pieces = pair, []
    for _ in range(PIECES):
        piece = rest.astype(np.float32).astype(ml_dtypes.bfloat16)
        pieces.append(piece)
        rest = rest - piece.astype(np.float64)
    return np.concatenate(pieces, 0)


def filter_chunk(x_ref, w_ref, first_channel, channels, write):
    _, beams, _, upchan, samples = x_ref.shape
    width = beams * samples
    count = w_ref.shape[1] // (2 * TAPS * upchan)
    time = lax.broadcasted_iota(jnp.int32, (upchan, width), 1) % samples
    for first in range(0, channels, count):
        tiles = []
        for channel in range(first, first + count):
            for part in range(2):
                signal = jnp.concatenate(
                    [x_ref[part, beam, first_channel + channel] for beam in range(beams)], axis=1
                )
                tiles.append(signal)
                signal = signal.astype(jnp.float32)
                for tap in range(1, TAPS):
                    moved = jnp.where(time >= tap, pltpu.roll(signal, tap, 1), 0.0)
                    tiles.append(moved.astype(jnp.bfloat16))
        stacked = jnp.concatenate(tiles, axis=0)
        spectrum = jnp.dot(w_ref[...], stacked, preferred_element_type=jnp.float32)
        rows = 2 * count * upchan
        total = spectrum[2 * rows :] + spectrum[rows : 2 * rows]
        total = total + spectrum[:rows]
        for offset in range(count):
            real = total[2 * offset * upchan : (2 * offset + 1) * upchan]
            imag = total[(2 * offset + 1) * upchan : (2 * offset + 2) * upchan]
            write(first + offset, (real * real + imag * imag).astype(jnp.bfloat16))


def exclusive_or(me, other, n):
    result = 0
    for bit in range(n.bit_length() - 1):
        result = result + (me // 2**bit % 2 + other // 2**bit % 2) % 2 * 2**bit
    return result


def table_places(me, level):
    size = 2**level
    base = me // (2 * size) * (2 * size)
    goals = [base + me % size * 2 + beam for beam in range(2)]
    origins = [base + me // 2 % size + slot * size for slot in range(2)]
    return goals, origins


def subband_kernel(
    n,
    x_hbm,
    w_hbm,
    delay_hbm,
    table_hbm,
    out_ref,
    x_ref,
    w_ref,
    delay_ref,
    table_ref,
    weights,
    level_tables,
    outgoing,
    arrived,
    local_delays,
    shifted,
    total,
    part,
    tables,
    send_sem,
    recv_sem,
    table_send,
    table_recv,
    input_sem,
    series,
    *merge_scratch,
):
    levels = n.bit_length() - 1
    me = lax.axis_index("freq")
    samples = x_ref.shape[4]
    _, each, upchan, width = arrived.shape
    rows, channels = delay_ref.shape
    groups, _, depth = local_delays.shape
    members = n // groups

    inputs = [
        pltpu.make_async_copy(source, goal, input_sem.at[place])
        for place, (source, goal) in enumerate(
            [(x_hbm, x_ref), (w_hbm, w_ref), (delay_hbm, delay_ref), (table_hbm, table_ref)]
        )
    ]
    for copy in inputs:
        copy.start()

    barrier = pltpu.get_barrier_semaphore()

    def greet(offset, carry):
        pl.semaphore_signal(
            barrier, inc=1, device_id={"freq": (me + offset) % n}, device_id_type=MESH
        )
        return carry

    lax.fori_loop(1, n, greet, 0)
    pl.semaphore_wait(barrier, n - 1)
    inputs[0].wait()
    inputs[1].wait()
    weights[...] = w_ref[...].astype(jnp.bfloat16)

    def table_copy(level, beam):
        goals, _ = table_places(me, level)
        slot = me // 2**level % 2
        return goals[beam], pltpu.make_async_remote_copy(
            src_ref=level_tables.at[level],
            dst_ref=tables.at[level, slot],
            send_sem=table_send.at[level, beam],
            recv_sem=table_recv.at[level, slot],
            device_id={"freq": goals[beam]},
            device_id_type=MESH,
        )

    def table_arrival(level, slot):
        _, origins = table_places(me, level)
        return origins[slot], pltpu.make_async_remote_copy(
            src_ref=level_tables.at[level],
            dst_ref=tables.at[level, slot],
            send_sem=table_send.at[level, 0],
            recv_sem=table_recv.at[level, slot],
            device_id={"freq": origins[slot]},
            device_id_type=MESH,
        )

    def chunk_copy(offset):
        return pltpu.make_async_remote_copy(
            src_ref=outgoing.at[offset],
            dst_ref=arrived.at[offset],
            send_sem=send_sem.at[offset],
            recv_sem=recv_sem.at[offset],
            device_id={"freq": exclusive_or(me, offset, n)},
            device_id_type=MESH,
        )

    def send_chunk(offset, carry):

        def write(index, tile):
            outgoing[offset, index] = tile

        filter_chunk(x_ref, weights, exclusive_or(me, offset, n) * each, each, write)
        chunk_copy(offset).start()
        return carry

    half = n // 2
    early = min(half + members, n)
    lax.fori_loop(half, early, send_chunk, 0)
    lax.fori_loop(1, half, send_chunk, 0)

    def write_own(index, tile):
        arrived[0, index] = tile

    filter_chunk(x_ref, weights, me * each, each, write_own)
    lax.fori_loop(early, n, send_chunk, 0)
    inputs[2].wait()
    inputs[3].wait()
    for level in range(levels):
        for row in range(3):
            level_tables[level, row : row + 1] = table_ref[row, level : level + 1]

    for level in range(levels):
        for beam in range(2):
            goal, copy = table_copy(level, beam)

            @pl.when(goal != me)
            def _():
                copy.start()

            @pl.when(goal == me)
            def _():
                tables[level, me // 2**level % 2] = level_tables[level]

    delays = delay_ref[...].astype(jnp.float32).astype(jnp.bfloat16)
    for group in range(groups):
        column = lax.broadcasted_iota(jnp.int32, (1, depth), 1)
        index, fine = column // upchan % each, column % upchan
        source = me ^ (group * members + column // (each * upchan))
        wanted = index * (n * upchan) + source * upchan + fine
        chosen = lax.broadcasted_iota(jnp.int32, (channels, depth), 0) == wanted
        chosen = jnp.where(chosen, 1.0, 0.0).astype(jnp.bfloat16)
        local_delays[group] = jnp.dot(
            delays, chosen, preferred_element_type=jnp.float32
        ).astype(jnp.int32)

    time = lax.broadcasted_iota(jnp.int32, (depth, width), 1) % samples
    inside = lax.broadcasted_iota(jnp.int32, (rows, width), 1) % samples >= STRIDE
    for group in range(groups):
        for offset in range(group * members, (group + 1) * members):
            if offset > 0:
                chunk_copy(offset).wait_recv()
        block = arrived[group * members : (group + 1) * members].reshape(depth, width)
        shifted[:depth] = block
        block = block.astype(jnp.float32)
        for shift in range(1, STRIDE):
            moved = jnp.where(time >= shift, pltpu.roll(block, shift, 1), 0.0)
            shifted[shift * depth : (shift + 1) * depth] = moved.astype(jnp.bfloat16)
        part[...] = jnp.zeros_like(part)

        def horner(step, carry):
            base = SHIFTS - STRIDE - STRIDE * step
            group_delays = local_delays[group]
            onehot = jnp.concatenate(
                [
                    jnp.where(group_delays == base + shift, 1.0, 0.0).astype(jnp.bfloat16)
                    for shift in range(STRIDE)
                ],
                axis=1,
            )
            term = jnp.dot(onehot, shifted[...], preferred_element_type=jnp.float32)
            part[...] = jnp.where(inside, pltpu.roll(part[...], STRIDE, 1), 0.0) + term
            return carry

        lax.fori_loop(0, SHIFTS // STRIDE, horner, 0)
        if group == 0:
            total[...] = part[...]
        elif group < groups - 1:
            total[...] += part[...]
    summed = total[...] + part[...] if groups > 1 else part[...]
    for beam in range(width // samples):
        series[beam] = summed[:, beam * samples : (beam + 1) * samples].T

    for level in range(levels):
        for slot in range(2):
            origin, arrival = table_arrival(level, slot)

            @pl.when(origin != me)
            def _():
                arrival.wait_recv()

        for beam in range(2):
            goal, copy = table_copy(level, beam)

            @pl.when(goal != me)
            def _():
                copy.wait_send()

    merge_series(n, series, tables, out_ref, *merge_scratch)

    def sent(offset, carry):
        chunk_copy(offset).wait_send()
        return carry

    lax.fori_loop(1, n, sent, 0)


def subbands(volts, delays, merge_tables, n):
    _, beams, coarse, upchan, samples = volts.shape
    rows, channels = delays.shape
    levels = n.bit_length() - 1
    each = coarse // n
    width = beams * samples
    piece = min(CROSS_SHIFT, samples)
    members = max(1, min(n, 256 // (each * upchan)))
    depth = members * each * upchan
    weights = jnp.asarray(filter_matrix(upchan, 2 if each % 2 == 0 else 1).astype(np.float32))
    merge_tables = merge_tables.transpose(1, 0, 2)
    return pl.pallas_call(
        functools.partial(subband_kernel, n),
        out_shape=jax.ShapeDtypeStruct((beams, WIDTHS, rows), jnp.float32),
        in_specs=[pl.BlockSpec(memory_space=pltpu.HBM)] * 4,
        out_specs=pl.BlockSpec(memory_space=pltpu.VMEM),
        scratch_shapes=[
            pltpu.VMEM(volts.shape, volts.dtype),
            pltpu.VMEM(weights.shape, weights.dtype),
            pltpu.VMEM(delays.shape, delays.dtype),
            pltpu.VMEM(merge_tables.shape, merge_tables.dtype),
            pltpu.VMEM(weights.shape, jnp.bfloat16),
            pltpu.VMEM((levels, 3, rows), jnp.int32),
            pltpu.VMEM((n, each, upchan, width), jnp.bfloat16),
            pltpu.VMEM((n, each, upchan, width), jnp.bfloat16),
            pltpu.VMEM((n // members, rows, depth), jnp.int32),
            pltpu.VMEM((STRIDE * depth, width), jnp.bfloat16),
            pltpu.VMEM((rows, width), jnp.float32),
            pltpu.VMEM((rows, width), jnp.float32),
            pltpu.VMEM((levels, 2, 3, rows), jnp.int32),
            pltpu.SemaphoreType.DMA((n,)),
            pltpu.SemaphoreType.DMA((n,)),
            pltpu.SemaphoreType.DMA((levels, 2)),
            pltpu.SemaphoreType.DMA((levels, 2)),
            pltpu.SemaphoreType.DMA((4,)),
            pltpu.VMEM((beams, samples, rows), jnp.float32),
            pltpu.VMEM((levels, samples, rows), jnp.float32),
            pltpu.VMEM((levels - 1, 2, samples, rows), jnp.float32),
            pltpu.VMEM((levels, piece, 2 * rows), jnp.float32),
            pltpu.VMEM((samples, 2 * rows), jnp.float32),
            pltpu.VMEM((2, WIDTHS, rows), jnp.float32),
            pltpu.VMEM((2, WIDTHS, rows), jnp.float32),
            pltpu.SemaphoreType.DMA((2, levels, samples // piece)),
            pltpu.SemaphoreType.DMA((2,)),
            pltpu.SemaphoreType.DMA((2,)),
        ],
        compiler_params=pltpu.CompilerParams(
            collective_id=0, has_side_effects=True, vmem_limit_bytes=VMEM_BYTES
        ),
        name="subbands",
    )(volts, weights, delays, merge_tables)


def later(series, amount):
    if amount % 8 == 0:
        zeros = jnp.zeros((amount, series.shape[1]), series.dtype)
        return jnp.concatenate([zeros, series[:-amount]], axis=0)
    time = lax.broadcasted_iota(jnp.int32, series.shape, 0)
    return jnp.where(time >= amount, pltpu.roll(series, amount, 0), 0.0)


def delayed(before, series, delays):
    count = series.shape[0]
    current = jnp.concatenate([before, series], axis=0)
    for bit in reversed(range(max(CROSS_SHIFT - 1, 1).bit_length())):
        amount = 2**bit
        chosen = (delays >> bit) & 1 == 1
        if amount >= 8:
            height = count + -(-(amount - 1) // 8) * 8
            first = current.shape[0] - height
            moved = current[first - amount : first - amount + height]
            current = jnp.where(chosen, moved, current[first:])
        else:
            current = jnp.where(chosen, pltpu.roll(current, amount, 0), current)
    return current[current.shape[0] - count :]


def permuted(series, index):
    samples, rows = series.shape
    lanes = min(LANES, rows)
    columns = []
    for first in range(0, index.shape[1], lanes):
        wanted = jnp.broadcast_to(index[:, first : first + lanes], (samples, lanes))
        place = wanted & (lanes - 1)
        result = None
        for start in range(0, rows, lanes):
            found = jnp.take_along_axis(
                series[:, start : start + lanes], place, axis=1, mode="promise_in_bounds"
            )
            result = found if start == 0 else jnp.where(wanted >= start, found, result)
        columns.append(result)
    return jnp.concatenate(columns, axis=1)


def merge_places(me, n):
    half = n // 2
    levels = n.bit_length() - 1
    partners = [me + (1 - 2 * (me // 2**level % 2)) * 2**level for level in range(levels)]
    goals = [slot * half + me // 2 for slot in range(2)]
    origins = [2 * (me % half) + beam for beam in range(2)]
    return partners, goals, origins


def merge_series(
    n, z_ref, table_ref, out_ref, taken, state, previous, final, peaks, landed, sems, end_send, end_recv
):
    levels = n.bit_length() - 1
    me = lax.axis_index("freq")
    partners, goals, origins = merge_places(me, n)
    samples, width = final.shape
    rows = width // 2
    piece = min(CROSS_SHIFT, samples)
    chunks = samples // piece

    def exchange(level, chunk):
        held = z_ref if level == 0 else state.at[level - 1]
        span = pl.ds(chunk * piece, piece)
        return pltpu.make_async_remote_copy(
            src_ref=held.at[1 - me // 2**level % 2, span],
            dst_ref=taken.at[level, span],
            send_sem=sems.at[0, level, chunk],
            recv_sem=sems.at[1, level, chunk],
            device_id={"freq": partners[level]},
            device_id_type=MESH,
        )

    def columns(level, row):
        return jnp.concatenate([table_ref[level, slot, row : row + 1] for slot in range(2)], axis=1)

    for chunk in range(chunks):
        exchange(0, chunk).start()
    for diagonal in range(levels + chunks - 1):
        for level in reversed(range(levels)):
            chunk = diagonal - level
            if not 0 <= chunk < chunks:
                continue
            span = slice(chunk * piece, (chunk + 1) * piece)
            bit = me // 2**level % 2
            kept = z_ref[bit, span] if level == 0 else state[level - 1, bit, span]
            exchange(level, chunk).wait_recv()
            other = taken[level, span]
            lower = jnp.where(bit == 0, kept, other)
            upper = jnp.where(bit == 0, other, kept)
            upper = permuted(upper, columns(level, 1))
            before = jnp.zeros_like(upper) if chunk == 0 else previous[level]
            if chunk < chunks - 1:
                previous[level] = upper
            merged = permuted(lower, columns(level, 0)) + delayed(before, upper, columns(level, 2))
            if level < levels - 1:
                state[level, 0, span] = merged[:, :rows]
                state[level, 1, span] = merged[:, rows:]
                exchange(level + 1, chunk).start()
            else:
                final[span] = merged

    final = final[...]
    centred = final - jnp.mean(final, axis=0, keepdims=True)
    boxcar = centred * lax.rsqrt(jnp.mean(centred * centred, axis=0, keepdims=True) + epsilon)
    maxima = [jnp.max(boxcar, axis=0, keepdims=True)]
    for count in range(1, WIDTHS):
        boxcar = boxcar + later(boxcar, 2 ** (count - 1))
        maxima.append(jnp.max(boxcar, axis=0, keepdims=True) / math.sqrt(2**count))
    maxima = jnp.concatenate(maxima, axis=0)
    beam = me % 2

    def send(slot):
        return pltpu.make_async_remote_copy(
            src_ref=peaks.at[slot],
            dst_ref=landed.at[beam],
            send_sem=end_send.at[slot],
            recv_sem=end_recv.at[beam],
            device_id={"freq": goals[slot]},
            device_id_type=MESH,
        )

    for slot in range(2):
        peaks[slot] = maxima[:, slot * rows : (slot + 1) * rows]
    for slot in range(2):

        @pl.when(goals[slot] != me)
        def _():
            send(slot).start()

        @pl.when(goals[slot] == me)
        def _():
            landed[beam] = peaks[slot]

    for slot in range(2):

        @pl.when(goals[slot] != me)
        def _():
            send(slot).wait_send()

    for source in range(2):

        @pl.when(origins[source] != me)
        def _():
            pltpu.make_async_remote_copy(
                src_ref=peaks.at[0],
                dst_ref=landed.at[source],
                send_sem=end_send.at[0],
                recv_sem=end_recv.at[source],
                device_id={"freq": origins[source]},
                device_id_type=MESH,
            ).wait_recv()

    out_ref[...] = landed[...]
    for level in range(levels):
        for chunk in range(chunks):
            exchange(level, chunk).wait_send()


def local(voltages, sub_delays, merge_tables):
    n = lax.axis_size("freq")
    return subbands(voltages, sub_delays, merge_tables, n)


def solution(mesh):
    return jax.shard_map(
        local,
        mesh=mesh,
        in_specs=(P(None, "beam", "freq", None, None), P("freq", None), P(None, None, "freq")),
        out_specs=P("beam", None, "freq"),
        check_vma=False,
    )
```

```python
import functools
import math

import jax
import jax.numpy as jnp
import ml_dtypes
import numpy as np
from jax import lax
from jax.experimental import pallas as pl
from jax.experimental.pallas import tpu as pltpu
from jax.sharding import PartitionSpec as P

TAPS = 4
WIDTHS = 8
SHIFTS = 32
LANES = 128
PIECE = 32
STRIDE = 4
CROSS_SHIFT = 64
PIECES = 3
VMEM_BYTES = 63 * 1024 * 1024
MESH = pl.DeviceIdType.MESH

epsilon = 1e-06


def filter_matrix(upchan, count):
    length = TAPS * upchan
    positions = np.arange(length, dtype=np.float64)
    window = np.sinc((positions - (length - 1) / 2.0) / upchan)
    window = window * (0.5 - 0.5 * np.cos(2.0 * math.pi * (positions + 0.5) / length))
    window = (window / np.sqrt(2.0 * np.sum(window * window))).reshape(TAPS, upchan)
    phase = np.arange(upchan)
    angle = 2.0 * math.pi * (phase[:, None] * phase[None, :] % upchan) / upchan
    cosine, sine = np.cos(angle), np.sin(angle)
    dft = np.stack([np.stack([cosine, sine], 1), np.stack([-sine, cosine], 1)], 0)
    full = dft[:, :, :, None, :] * window[None, None, None]
    full = full.reshape(2 * upchan, 2 * TAPS * upchan)
    pair = np.zeros((count, 2 * upchan, count, 2 * TAPS * upchan))
    for channel in range(count):
        pair[channel, :, channel] = full
    pair = pair.reshape(2 * count * upchan, 2 * count * TAPS * upchan)
    rest, pieces = pair, []
    for _ in range(PIECES):
        piece = rest.astype(np.float32).astype(ml_dtypes.bfloat16)
        pieces.append(piece)
        rest = rest - piece.astype(np.float64)
    return np.concatenate(pieces, 0)


def filter_chunk(x_ref, w_ref, first_channel, channels, write):
    _, beams, _, upchan, samples = x_ref.shape
    width = beams * samples
    count = w_ref.shape[1] // (2 * TAPS * upchan)
    time = lax.broadcasted_iota(jnp.int32, (upchan, width), 1) % samples
    for first in range(0, channels, count):
        tiles = []
        for channel in range(first, first + count):
            for part in range(2):
                signal = jnp.concatenate(
                    [x_ref[part, beam, first_channel + channel] for beam in range(beams)], axis=1
                )
                tiles.append(signal)
                signal = signal.astype(jnp.float32)
                for tap in range(1, TAPS):
                    moved = jnp.where(time >= tap, pltpu.roll(signal, tap, 1), 0.0)
                    tiles.append(moved.astype(jnp.bfloat16))
        stacked = jnp.concatenate(tiles, axis=0)
        spectrum = jnp.dot(w_ref[...], stacked, preferred_element_type=jnp.float32)
        rows = 2 * count * upchan
        total = spectrum[2 * rows :] + spectrum[rows : 2 * rows]
        total = total + spectrum[:rows]
        for offset in range(count):
            real = total[2 * offset * upchan : (2 * offset + 1) * upchan]
            imag = total[(2 * offset + 1) * upchan : (2 * offset + 2) * upchan]
            write(first + offset, (real * real + imag * imag).astype(jnp.bfloat16))


def exclusive_or(me, other, n):
    result = 0
    for bit in range(n.bit_length() - 1):
        result = result + (me // 2**bit % 2 + other // 2**bit % 2) % 2 * 2**bit
    return result


def table_places(me, level):
    size = 2**level
    base = me // (2 * size) * (2 * size)
    goals = [base + me % size * 2 + beam for beam in range(2)]
    origins = [base + me // 2 % size + slot * size for slot in range(2)]
    return goals, origins


def subband_kernel(
    n,
    x_hbm,
    w_hbm,
    delay_hbm,
    table_hbm,
    out_ref,
    x_ref,
    w_ref,
    delay_ref,
    table_ref,
    weights,
    level_tables,
    outgoing,
    arrived,
    local_delays,
    shifted,
    total,
    part,
    tables,
    send_sem,
    recv_sem,
    table_send,
    table_recv,
    input_sem,
    series,
    *merge_scratch,
):
    levels = n.bit_length() - 1
    me = lax.axis_index("freq")
    samples = x_ref.shape[4]
    _, each, upchan, width = arrived.shape
    rows, channels = delay_ref.shape
    groups, _, depth = local_delays.shape
    members = n // groups

    inputs = [
        pltpu.make_async_copy(source, goal, input_sem.at[place])
        for place, (source, goal) in enumerate(
            [(x_hbm, x_ref), (w_hbm, w_ref), (delay_hbm, delay_ref), (table_hbm, table_ref)]
        )
    ]
    for copy in inputs:
        copy.start()

    barrier = pltpu.get_barrier_semaphore()

    def greet(offset, carry):
        pl.semaphore_signal(
            barrier, inc=1, device_id={"freq": (me + offset) % n}, device_id_type=MESH
        )
        return carry

    lax.fori_loop(1, n, greet, 0)
    pl.semaphore_wait(barrier, n - 1)
    inputs[0].wait()
    inputs[1].wait()
    weights[...] = w_ref[...].astype(jnp.bfloat16)

    def table_copy(level, beam):
        goals, _ = table_places(me, level)
        slot = me // 2**level % 2
        return goals[beam], pltpu.make_async_remote_copy(
            src_ref=level_tables.at[level],
            dst_ref=tables.at[level, slot],
            send_sem=table_send.at[level, beam],
            recv_sem=table_recv.at[level, slot],
            device_id={"freq": goals[beam]},
            device_id_type=MESH,
        )

    def table_arrival(level, slot):
        _, origins = table_places(me, level)
        return origins[slot], pltpu.make_async_remote_copy(
            src_ref=level_tables.at[level],
            dst_ref=tables.at[level, slot],
            send_sem=table_send.at[level, 0],
            recv_sem=table_recv.at[level, slot],
            device_id={"freq": origins[slot]},
            device_id_type=MESH,
        )

    def chunk_copy(offset):
        return pltpu.make_async_remote_copy(
            src_ref=outgoing.at[offset],
            dst_ref=arrived.at[offset],
            send_sem=send_sem.at[offset],
            recv_sem=recv_sem.at[offset],
            device_id={"freq": exclusive_or(me, offset, n)},
            device_id_type=MESH,
        )

    def send_chunk(offset, carry):

        def write(index, tile):
            outgoing[offset, index] = tile

        filter_chunk(x_ref, weights, exclusive_or(me, offset, n) * each, each, write)
        chunk_copy(offset).start()
        return carry

    half = n // 2
    early = min(half + members, n)
    lax.fori_loop(half, early, send_chunk, 0)
    lax.fori_loop(1, half, send_chunk, 0)

    def write_own(index, tile):
        arrived[0, index] = tile

    filter_chunk(x_ref, weights, me * each, each, write_own)
    lax.fori_loop(early, n, send_chunk, 0)
    inputs[2].wait()
    inputs[3].wait()
    for level in range(levels):
        for row in range(3):
            level_tables[level, row : row + 1] = table_ref[row, level : level + 1]

    for level in range(levels):
        for beam in range(2):
            goal, copy = table_copy(level, beam)

            @pl.when(goal != me)
            def _():
                copy.start()

            @pl.when(goal == me)
            def _():
                tables[level, me // 2**level % 2] = level_tables[level]

    delays = delay_ref[...].astype(jnp.float32).astype(jnp.bfloat16)
    for group in range(groups):
        column = lax.broadcasted_iota(jnp.int32, (1, depth), 1)
        index, fine = column // upchan % each, column % upchan
        source = me ^ (group * members + column // (each * upchan))
        wanted = index * (n * upchan) + source * upchan + fine
        chosen = lax.broadcasted_iota(jnp.int32, (channels, depth), 0) == wanted
        chosen = jnp.where(chosen, 1.0, 0.0).astype(jnp.bfloat16)
        local_delays[group] = jnp.dot(
            delays, chosen, preferred_element_type=jnp.float32
        ).astype(jnp.int32)

    time = lax.broadcasted_iota(jnp.int32, (depth, width), 1) % samples
    inside = lax.broadcasted_iota(jnp.int32, (rows, width), 1) % samples >= STRIDE
    for group in range(groups):
        for offset in range(group * members, (group + 1) * members):
            if offset > 0:
                chunk_copy(offset).wait_recv()
        block = arrived[group * members : (group + 1) * members].reshape(depth, width)
        shifted[:depth] = block
        block = block.astype(jnp.float32)
        for shift in range(1, STRIDE):
            moved = jnp.where(time >= shift, pltpu.roll(block, shift, 1), 0.0)
            shifted[shift * depth : (shift + 1) * depth] = moved.astype(jnp.bfloat16)
        part[...] = jnp.zeros_like(part)

        def horner(step, carry):
            base = SHIFTS - STRIDE - STRIDE * step
            group_delays = local_delays[group]
            onehot = jnp.concatenate(
                [
                    jnp.where(group_delays == base + shift, 1.0, 0.0).astype(jnp.bfloat16)
                    for shift in range(STRIDE)
                ],
                axis=1,
            )
            term = jnp.dot(onehot, shifted[...], preferred_element_type=jnp.float32)
            part[...] = jnp.where(inside, pltpu.roll(part[...], STRIDE, 1), 0.0) + term
            return carry

        lax.fori_loop(0, SHIFTS // STRIDE, horner, 0)
        if group == 0:
            total[...] = part[...]
        elif group < groups - 1:
            total[...] += part[...]
    summed = total[...] + part[...] if groups > 1 else part[...]
    for beam in range(width // samples):
        series[beam] = summed[:, beam * samples : (beam + 1) * samples].T

    for level in range(levels):
        for slot in range(2):
            origin, arrival = table_arrival(level, slot)

            @pl.when(origin != me)
            def _():
                arrival.wait_recv()

        for beam in range(2):
            goal, copy = table_copy(level, beam)

            @pl.when(goal != me)
            def _():
                copy.wait_send()

    merge_series(n, series, tables, out_ref, *merge_scratch)

    def sent(offset, carry):
        chunk_copy(offset).wait_send()
        return carry

    lax.fori_loop(1, n, sent, 0)


def subbands(volts, delays, merge_tables, n):
    _, beams, coarse, upchan, samples = volts.shape
    rows, channels = delays.shape
    levels = n.bit_length() - 1
    each = coarse // n
    width = beams * samples
    piece = min(PIECE, samples)
    members = max(1, min(n, 256 // (each * upchan)))
    depth = members * each * upchan
    weights = jnp.asarray(filter_matrix(upchan, 2 if each % 2 == 0 else 1).astype(np.float32))
    merge_tables = merge_tables.transpose(1, 0, 2)
    return pl.pallas_call(
        functools.partial(subband_kernel, n),
        out_shape=jax.ShapeDtypeStruct((beams, WIDTHS, rows), jnp.float32),
        in_specs=[pl.BlockSpec(memory_space=pltpu.HBM)] * 4,
        out_specs=pl.BlockSpec(memory_space=pltpu.VMEM),
        scratch_shapes=[
            pltpu.VMEM(volts.shape, volts.dtype),
            pltpu.VMEM(weights.shape, weights.dtype),
            pltpu.VMEM(delays.shape, delays.dtype),
            pltpu.VMEM(merge_tables.shape, merge_tables.dtype),
            pltpu.VMEM(weights.shape, jnp.bfloat16),
            pltpu.VMEM((levels, 3, rows), jnp.int32),
            pltpu.VMEM((n, each, upchan, width), jnp.bfloat16),
            pltpu.VMEM((n, each, upchan, width), jnp.bfloat16),
            pltpu.VMEM((n // members, rows, depth), jnp.int32),
            pltpu.VMEM((STRIDE * depth, width), jnp.bfloat16),
            pltpu.VMEM((rows, width), jnp.float32),
            pltpu.VMEM((rows, width), jnp.float32),
            pltpu.VMEM((levels, 2, 3, rows), jnp.int32),
            pltpu.SemaphoreType.DMA((n,)),
            pltpu.SemaphoreType.DMA((n,)),
            pltpu.SemaphoreType.DMA((levels, 2)),
            pltpu.SemaphoreType.DMA((levels, 2)),
            pltpu.SemaphoreType.DMA((4,)),
            pltpu.VMEM((beams, samples, rows), jnp.float32),
            pltpu.VMEM((levels, samples, rows), jnp.float32),
            pltpu.VMEM((levels - 1, 2, samples, rows), jnp.float32),
            pltpu.VMEM((levels, CROSS_SHIFT, 2 * rows), jnp.float32),
            pltpu.VMEM((samples, 2 * rows), jnp.float32),
            pltpu.VMEM((2, WIDTHS, rows), jnp.float32),
            pltpu.VMEM((2, WIDTHS, rows), jnp.float32),
            pltpu.SemaphoreType.DMA((2, levels, samples // piece)),
            pltpu.SemaphoreType.DMA((2,)),
            pltpu.SemaphoreType.DMA((2,)),
        ],
        compiler_params=pltpu.CompilerParams(
            collective_id=0, has_side_effects=True, vmem_limit_bytes=VMEM_BYTES
        ),
        name="subbands",
    )(volts, weights, delays, merge_tables)


def later(series, amount):
    if amount % 8 == 0:
        zeros = jnp.zeros((amount, series.shape[1]), series.dtype)
        return jnp.concatenate([zeros, series[:-amount]], axis=0)
    time = lax.broadcasted_iota(jnp.int32, series.shape, 0)
    return jnp.where(time >= amount, pltpu.roll(series, amount, 0), 0.0)


def delayed(before, series, delays):
    count = series.shape[0]
    current = jnp.concatenate([before, series], axis=0)
    for bit in reversed(range(max(CROSS_SHIFT - 1, 1).bit_length())):
        amount = 2**bit
        chosen = (delays >> bit) & 1 == 1
        if amount >= 8:
            height = count + -(-(amount - 1) // 8) * 8
            first = current.shape[0] - height
            moved = current[first - amount : first - amount + height]
            current = jnp.where(chosen, moved, current[first:])
        else:
            current = jnp.where(chosen, pltpu.roll(current, amount, 0), current)
    return current[current.shape[0] - count :]


def permuted(series, index):
    samples, rows = series.shape
    lanes = min(LANES, rows)
    columns = []
    for first in range(0, index.shape[1], lanes):
        wanted = jnp.broadcast_to(index[:, first : first + lanes], (samples, lanes))
        place = wanted & (lanes - 1)
        result = None
        for start in range(0, rows, lanes):
            found = jnp.take_along_axis(
                series[:, start : start + lanes], place, axis=1, mode="promise_in_bounds"
            )
            result = found if start == 0 else jnp.where(wanted >= start, found, result)
        columns.append(result)
    return jnp.concatenate(columns, axis=1)


def merge_places(me, n):
    half = n // 2
    levels = n.bit_length() - 1
    partners = [me + (1 - 2 * (me // 2**level % 2)) * 2**level for level in range(levels)]
    goals = [slot * half + me // 2 for slot in range(2)]
    origins = [2 * (me % half) + beam for beam in range(2)]
    return partners, goals, origins


def chunk_order(levels, chunks):
    expected = {}
    for level in range(levels):
        wire = 0.2 if level == 0 else 1.3 if level == levels - 1 else 0.65
        delay = 0.5 if level == 0 else 1.0
        free = 0.0
        for chunk in range(chunks):
            ready = expected[level - 1, chunk] + 0.25 if level else 0.0
            free = max(free, ready) + wire
            expected[level, chunk] = free + delay
    return sorted(expected, key=lambda step: (expected[step], step))


def merge_series(
    n, z_ref, table_ref, out_ref, taken, state, previous, final, peaks, landed, sems, end_send, end_recv
):
    levels = n.bit_length() - 1
    me = lax.axis_index("freq")
    partners, goals, origins = merge_places(me, n)
    samples, width = final.shape
    rows = width // 2
    piece = min(PIECE, samples)
    chunks = samples // piece

    def exchange(level, chunk):
        held = z_ref if level == 0 else state.at[level - 1]
        span = pl.ds(chunk * piece, piece)
        return pltpu.make_async_remote_copy(
            src_ref=held.at[1 - me // 2**level % 2, span],
            dst_ref=taken.at[level, span],
            send_sem=sems.at[0, level, chunk],
            recv_sem=sems.at[1, level, chunk],
            device_id={"freq": partners[level]},
            device_id_type=MESH,
        )

    def columns(level, row):
        return jnp.concatenate([table_ref[level, slot, row : row + 1] for slot in range(2)], axis=1)

    for chunk in range(chunks):
        exchange(0, chunk).start()
    for level, chunk in chunk_order(levels, chunks):
        span = slice(chunk * piece, (chunk + 1) * piece)
        bit = me // 2**level % 2
        kept = z_ref[bit, span] if level == 0 else state[level - 1, bit, span]
        exchange(level, chunk).wait_recv()
        other = taken[level, span]
        lower = jnp.where(bit == 0, kept, other)
        upper = jnp.where(bit == 0, other, kept)
        upper = permuted(upper, columns(level, 1))
        before = jnp.zeros((CROSS_SHIFT, width), jnp.float32) if chunk == 0 else previous[level]
        if chunk < chunks - 1:
            previous[level] = jnp.concatenate([before, upper], axis=0)[-CROSS_SHIFT:]
        merged = permuted(lower, columns(level, 0)) + delayed(before, upper, columns(level, 2))
        if level < levels - 1:
            state[level, 0, span] = merged[:, :rows]
            state[level, 1, span] = merged[:, rows:]
            exchange(level + 1, chunk).start()
        else:
            final[span] = merged

    final = final[...]
    centred = final - jnp.mean(final, axis=0, keepdims=True)
    boxcar = centred * lax.rsqrt(jnp.mean(centred * centred, axis=0, keepdims=True) + epsilon)
    maxima = [jnp.max(boxcar, axis=0, keepdims=True)]
    for count in range(1, WIDTHS):
        boxcar = boxcar + later(boxcar, 2 ** (count - 1))
        maxima.append(jnp.max(boxcar, axis=0, keepdims=True) / math.sqrt(2**count))
    maxima = jnp.concatenate(maxima, axis=0)
    beam = me % 2

    def send(slot):
        return pltpu.make_async_remote_copy(
            src_ref=peaks.at[slot],
            dst_ref=landed.at[beam],
            send_sem=end_send.at[slot],
            recv_sem=end_recv.at[beam],
            device_id={"freq": goals[slot]},
            device_id_type=MESH,
        )

    for slot in range(2):
        peaks[slot] = maxima[:, slot * rows : (slot + 1) * rows]
    for slot in range(2):

        @pl.when(goals[slot] != me)
        def _():
            send(slot).start()

        @pl.when(goals[slot] == me)
        def _():
            landed[beam] = peaks[slot]

    for slot in range(2):

        @pl.when(goals[slot] != me)
        def _():
            send(slot).wait_send()

    for source in range(2):

        @pl.when(origins[source] != me)
        def _():
            pltpu.make_async_remote_copy(
                src_ref=peaks.at[0],
                dst_ref=landed.at[source],
                send_sem=end_send.at[0],
                recv_sem=end_recv.at[source],
                device_id={"freq": origins[source]},
                device_id_type=MESH,
            ).wait_recv()

    out_ref[...] = landed[...]
    for level in range(levels):
        for chunk in range(chunks):
            exchange(level, chunk).wait_send()


def local(voltages, sub_delays, merge_tables):
    n = lax.axis_size("freq")
    return subbands(voltages, sub_delays, merge_tables, n)


def solution(mesh):
    return jax.shard_map(
        local,
        mesh=mesh,
        in_specs=(P(None, "beam", "freq", None, None), P("freq", None), P(None, None, "freq")),
        out_specs=P("beam", None, "freq"),
        check_vma=False,
    )
```

```python
import functools
import math

import jax
import jax.numpy as jnp
import ml_dtypes
import numpy as np
from jax import lax
from jax.experimental import pallas as pl
from jax.experimental.pallas import tpu as pltpu
from jax.sharding import PartitionSpec as P

TAPS = 4
WIDTHS = 8
SHIFTS = 32
LANES = 128
PIECE = 32
STRIDE = 4
CROSS_SHIFT = 64
PIECES = 3
VMEM_BYTES = 63 * 1024 * 1024
MESH = pl.DeviceIdType.MESH

epsilon = 1e-06


def filter_matrix(upchan, count):
    length = TAPS * upchan
    positions = np.arange(length, dtype=np.float64)
    window = np.sinc((positions - (length - 1) / 2.0) / upchan)
    window = window * (0.5 - 0.5 * np.cos(2.0 * math.pi * (positions + 0.5) / length))
    window = (window / np.sqrt(2.0 * np.sum(window * window))).reshape(TAPS, upchan)
    phase = np.arange(upchan)
    angle = 2.0 * math.pi * (phase[:, None] * phase[None, :] % upchan) / upchan
    cosine, sine = np.cos(angle), np.sin(angle)
    dft = np.stack([np.stack([cosine, sine], 1), np.stack([-sine, cosine], 1)], 0)
    full = dft[:, :, :, None, :] * window[None, None, None]
    full = full.reshape(2 * upchan, 2 * TAPS * upchan)
    pair = np.zeros((count, 2 * upchan, count, 2 * TAPS * upchan))
    for channel in range(count):
        pair[channel, :, channel] = full
    pair = pair.reshape(2 * count * upchan, 2 * count * TAPS * upchan)
    rest, pieces = pair, []
    for _ in range(PIECES):
        piece = rest.astype(np.float32).astype(ml_dtypes.bfloat16)
        pieces.append(piece)
        rest = rest - piece.astype(np.float64)
    return np.concatenate(pieces, 0)


def filter_chunk(x_ref, w_ref, first_channel, channels, write):
    _, beams, _, upchan, samples = x_ref.shape
    width = beams * samples
    count = w_ref.shape[1] // (2 * TAPS * upchan)
    time = lax.broadcasted_iota(jnp.int32, (upchan, width), 1) % samples
    for first in range(0, channels, count):
        tiles = []
        for channel in range(first, first + count):
            for part in range(2):
                signal = jnp.concatenate(
                    [x_ref[part, beam, first_channel + channel] for beam in range(beams)], axis=1
                )
                tiles.append(signal)
                signal = signal.astype(jnp.float32)
                for tap in range(1, TAPS):
                    moved = jnp.where(time >= tap, pltpu.roll(signal, tap, 1), 0.0)
                    tiles.append(moved.astype(jnp.bfloat16))
        stacked = jnp.concatenate(tiles, axis=0)
        spectrum = jnp.dot(w_ref[...], stacked, preferred_element_type=jnp.float32)
        rows = 2 * count * upchan
        total = spectrum[2 * rows :] + spectrum[rows : 2 * rows]
        total = total + spectrum[:rows]
        for offset in range(count):
            real = total[2 * offset * upchan : (2 * offset + 1) * upchan]
            imag = total[(2 * offset + 1) * upchan : (2 * offset + 2) * upchan]
            write(first + offset, (real * real + imag * imag).astype(jnp.bfloat16))


def exclusive_or(me, other, n):
    result = 0
    for bit in range(n.bit_length() - 1):
        result = result + (me // 2**bit % 2 + other // 2**bit % 2) % 2 * 2**bit
    return result


def table_places(me, level):
    size = 2**level
    base = me // (2 * size) * (2 * size)
    goals = [base + me % size * 2 + beam for beam in range(2)]
    origins = [base + me // 2 % size + slot * size for slot in range(2)]
    return goals, origins


def subband_kernel(
    n,
    x_hbm,
    w_hbm,
    delay_hbm,
    table_hbm,
    out_ref,
    x_ref,
    w_ref,
    delay_ref,
    table_ref,
    weights,
    level_tables,
    outgoing,
    arrived,
    local_delays,
    shifted,
    total,
    part,
    tables,
    send_sem,
    recv_sem,
    table_send,
    table_recv,
    input_sem,
    series,
    *merge_scratch,
):
    levels = n.bit_length() - 1
    me = lax.axis_index("freq")
    samples = x_ref.shape[4]
    _, each, upchan, width = arrived.shape
    rows, channels = delay_ref.shape
    groups, _, depth = local_delays.shape
    members = n // groups

    inputs = [
        pltpu.make_async_copy(source, goal, input_sem.at[place])
        for place, (source, goal) in enumerate(
            [(x_hbm, x_ref), (w_hbm, w_ref), (delay_hbm, delay_ref), (table_hbm, table_ref)]
        )
    ]
    for copy in inputs:
        copy.start()

    barrier = pltpu.get_barrier_semaphore()

    def greet(offset, carry):
        pl.semaphore_signal(
            barrier, inc=1, device_id={"freq": (me + offset) % n}, device_id_type=MESH
        )
        return carry

    lax.fori_loop(1, n, greet, 0)
    pl.semaphore_wait(barrier, n - 1)
    inputs[0].wait()
    inputs[1].wait()
    weights[...] = w_ref[...].astype(jnp.bfloat16)

    def table_copy(level, beam):
        goals, _ = table_places(me, level)
        slot = me // 2**level % 2
        return goals[beam], pltpu.make_async_remote_copy(
            src_ref=level_tables.at[level],
            dst_ref=tables.at[level, slot],
            send_sem=table_send.at[level, beam],
            recv_sem=table_recv.at[level, slot],
            device_id={"freq": goals[beam]},
            device_id_type=MESH,
        )

    def table_arrival(level, slot):
        _, origins = table_places(me, level)
        return origins[slot], pltpu.make_async_remote_copy(
            src_ref=level_tables.at[level],
            dst_ref=tables.at[level, slot],
            send_sem=table_send.at[level, 0],
            recv_sem=table_recv.at[level, slot],
            device_id={"freq": origins[slot]},
            device_id_type=MESH,
        )

    def chunk_copy(offset):
        return pltpu.make_async_remote_copy(
            src_ref=outgoing.at[offset],
            dst_ref=arrived.at[offset],
            send_sem=send_sem.at[offset],
            recv_sem=recv_sem.at[offset],
            device_id={"freq": exclusive_or(me, offset, n)},
            device_id_type=MESH,
        )

    def send_chunk(offset, carry):

        def write(index, tile):
            outgoing[offset, index] = tile

        filter_chunk(x_ref, weights, exclusive_or(me, offset, n) * each, each, write)
        chunk_copy(offset).start()
        return carry

    half = n // 2
    early = min(half + members, n)
    lax.fori_loop(half, early, send_chunk, 0)
    lax.fori_loop(1, half, send_chunk, 0)

    def write_own(index, tile):
        arrived[0, index] = tile

    filter_chunk(x_ref, weights, me * each, each, write_own)
    lax.fori_loop(early, n, send_chunk, 0)
    inputs[2].wait()
    inputs[3].wait()
    for level in range(levels):
        for row in range(3):
            level_tables[level, row : row + 1] = table_ref[row, level : level + 1]

    for level in range(levels):
        for beam in range(2):
            goal, copy = table_copy(level, beam)

            @pl.when(goal != me)
            def _():
                copy.start()

            @pl.when(goal == me)
            def _():
                tables[level, me // 2**level % 2] = level_tables[level]

    delays = delay_ref[...].astype(jnp.float32).astype(jnp.bfloat16)
    for group in range(groups):
        column = lax.broadcasted_iota(jnp.int32, (1, depth), 1)
        index, fine = column // upchan % each, column % upchan
        source = me ^ (group * members + column // (each * upchan))
        wanted = index * (n * upchan) + source * upchan + fine
        chosen = lax.broadcasted_iota(jnp.int32, (channels, depth), 0) == wanted
        chosen = jnp.where(chosen, 1.0, 0.0).astype(jnp.bfloat16)
        local_delays[group] = jnp.dot(
            delays, chosen, preferred_element_type=jnp.float32
        ).astype(jnp.bfloat16)

    time = lax.broadcasted_iota(jnp.int32, (depth, width), 1) % samples
    inside = lax.broadcasted_iota(jnp.int32, (rows, width), 1) % samples >= STRIDE
    for group in range(groups):
        for offset in range(group * members, (group + 1) * members):
            if offset > 0:
                chunk_copy(offset).wait_recv()
        block = arrived[group * members : (group + 1) * members].reshape(depth, width)
        shifted[:depth] = block
        block = block.astype(jnp.float32)
        for shift in range(1, STRIDE):
            moved = jnp.where(time >= shift, pltpu.roll(block, shift, 1), 0.0)
            shifted[shift * depth : (shift + 1) * depth] = moved.astype(jnp.bfloat16)
        part[...] = jnp.zeros_like(part)

        def horner(step, carry):
            base = (SHIFTS - STRIDE - STRIDE * step).astype(jnp.float32)
            one, zero = jnp.bfloat16(1.0), jnp.bfloat16(0.0)
            group_delays = local_delays[group]
            onehot = jnp.concatenate(
                [
                    jnp.where(group_delays == (base + shift).astype(jnp.bfloat16), one, zero)
                    for shift in range(STRIDE)
                ],
                axis=1,
            )
            term = jnp.dot(onehot, shifted[...], preferred_element_type=jnp.float32)
            part[...] = jnp.where(inside, pltpu.roll(part[...], STRIDE, 1), 0.0) + term
            return carry

        lax.fori_loop(0, SHIFTS // STRIDE, horner, 0)
        if group == 0:
            total[...] = part[...]
        elif group < groups - 1:
            total[...] += part[...]
    summed = total[...] + part[...] if groups > 1 else part[...]
    for beam in range(width // samples):
        series[beam] = summed[:, beam * samples : (beam + 1) * samples].T

    for level in range(levels):
        for slot in range(2):
            origin, arrival = table_arrival(level, slot)

            @pl.when(origin != me)
            def _():
                arrival.wait_recv()

        for beam in range(2):
            goal, copy = table_copy(level, beam)

            @pl.when(goal != me)
            def _():
                copy.wait_send()

    merge_series(n, series, tables, out_ref, *merge_scratch)

    def sent(offset, carry):
        chunk_copy(offset).wait_send()
        return carry

    lax.fori_loop(1, n, sent, 0)


def subbands(volts, delays, merge_tables, n):
    _, beams, coarse, upchan, samples = volts.shape
    rows, channels = delays.shape
    levels = n.bit_length() - 1
    each = coarse // n
    width = beams * samples
    piece = min(PIECE, samples)
    members = max(1, min(n, 256 // (each * upchan)))
    depth = members * each * upchan
    weights = jnp.asarray(filter_matrix(upchan, 2 if each % 2 == 0 else 1).astype(np.float32))
    merge_tables = merge_tables.transpose(1, 0, 2)
    return pl.pallas_call(
        functools.partial(subband_kernel, n),
        out_shape=jax.ShapeDtypeStruct((beams, WIDTHS, rows), jnp.float32),
        in_specs=[pl.BlockSpec(memory_space=pltpu.HBM)] * 4,
        out_specs=pl.BlockSpec(memory_space=pltpu.VMEM),
        scratch_shapes=[
            pltpu.VMEM(volts.shape, volts.dtype),
            pltpu.VMEM(weights.shape, weights.dtype),
            pltpu.VMEM(delays.shape, delays.dtype),
            pltpu.VMEM(merge_tables.shape, merge_tables.dtype),
            pltpu.VMEM(weights.shape, jnp.bfloat16),
            pltpu.VMEM((levels, 3, rows), jnp.int32),
            pltpu.VMEM((n, each, upchan, width), jnp.bfloat16),
            pltpu.VMEM((n, each, upchan, width), jnp.bfloat16),
            pltpu.VMEM((n // members, rows, depth), jnp.bfloat16),
            pltpu.VMEM((STRIDE * depth, width), jnp.bfloat16),
            pltpu.VMEM((rows, width), jnp.float32),
            pltpu.VMEM((rows, width), jnp.float32),
            pltpu.VMEM((levels, 2, 3, rows), jnp.int32),
            pltpu.SemaphoreType.DMA((n,)),
            pltpu.SemaphoreType.DMA((n,)),
            pltpu.SemaphoreType.DMA((levels, 2)),
            pltpu.SemaphoreType.DMA((levels, 2)),
            pltpu.SemaphoreType.DMA((4,)),
            pltpu.VMEM((beams, samples, rows), jnp.float32),
            pltpu.VMEM((levels, samples, rows), jnp.float32),
            pltpu.VMEM((levels - 1, 2, samples, rows), jnp.float32),
            pltpu.VMEM((levels, CROSS_SHIFT, 2 * rows), jnp.float32),
            pltpu.VMEM((samples, 2 * rows), jnp.float32),
            pltpu.VMEM((2, WIDTHS, rows), jnp.float32),
            pltpu.VMEM((2, WIDTHS, rows), jnp.float32),
            pltpu.SemaphoreType.DMA((2, levels, samples // piece)),
            pltpu.SemaphoreType.DMA((2,)),
            pltpu.SemaphoreType.DMA((2,)),
        ],
        compiler_params=pltpu.CompilerParams(
            collective_id=0, has_side_effects=True, vmem_limit_bytes=VMEM_BYTES
        ),
        name="subbands",
    )(volts, weights, delays, merge_tables)


def later(series, amount):
    if amount % 8 == 0:
        zeros = jnp.zeros((amount, series.shape[1]), series.dtype)
        return jnp.concatenate([zeros, series[:-amount]], axis=0)
    time = lax.broadcasted_iota(jnp.int32, series.shape, 0)
    return jnp.where(time >= amount, pltpu.roll(series, amount, 0), 0.0)


def delayed(before, series, delays):
    count = series.shape[0]
    current = jnp.concatenate([before, series], axis=0)
    for bit in reversed(range(max(CROSS_SHIFT - 1, 1).bit_length())):
        amount = 2**bit
        chosen = (delays >> bit) & 1 == 1
        if amount >= 8:
            height = count + -(-(amount - 1) // 8) * 8
            first = current.shape[0] - height
            moved = current[first - amount : first - amount + height]
            current = jnp.where(chosen, moved, current[first:])
        else:
            current = jnp.where(chosen, pltpu.roll(current, amount, 0), current)
    return current[current.shape[0] - count :]


def permuted(series, index):
    samples, rows = series.shape
    lanes = min(LANES, rows)
    columns = []
    for first in range(0, index.shape[1], lanes):
        wanted = jnp.broadcast_to(index[:, first : first + lanes], (samples, lanes))
        place = wanted & (lanes - 1)
        result = None
        for start in range(0, rows, lanes):
            found = jnp.take_along_axis(
                series[:, start : start + lanes], place, axis=1, mode="promise_in_bounds"
            )
            result = found if start == 0 else jnp.where(wanted >= start, found, result)
        columns.append(result)
    return jnp.concatenate(columns, axis=1)


def merge_places(me, n):
    half = n // 2
    levels = n.bit_length() - 1
    partners = [me + (1 - 2 * (me // 2**level % 2)) * 2**level for level in range(levels)]
    goals = [slot * half + me // 2 for slot in range(2)]
    origins = [2 * (me % half) + beam for beam in range(2)]
    return partners, goals, origins


def chunk_order(levels, chunks):
    expected = {}
    for level in range(levels):
        wire = 0.2 if level == 0 else 1.3 if level == levels - 1 else 0.65
        delay = 0.5 if level == 0 else 1.0
        free = 0.0
        for chunk in range(chunks):
            ready = expected[level - 1, chunk] + 0.25 if level else 0.0
            free = max(free, ready) + wire
            expected[level, chunk] = free + delay
    return sorted(expected, key=lambda step: (expected[step], step))


def merge_series(
    n, z_ref, table_ref, out_ref, taken, state, previous, final, peaks, landed, sems, end_send, end_recv
):
    levels = n.bit_length() - 1
    me = lax.axis_index("freq")
    partners, goals, origins = merge_places(me, n)
    samples, width = final.shape
    rows = width // 2
    piece = min(PIECE, samples)
    chunks = samples // piece

    def exchange(level, chunk):
        held = z_ref if level == 0 else state.at[level - 1]
        span = pl.ds(chunk * piece, piece)
        return pltpu.make_async_remote_copy(
            src_ref=held.at[1 - me // 2**level % 2, span],
            dst_ref=taken.at[level, span],
            send_sem=sems.at[0, level, chunk],
            recv_sem=sems.at[1, level, chunk],
            device_id={"freq": partners[level]},
            device_id_type=MESH,
        )

    def columns(level, row):
        return jnp.concatenate([table_ref[level, slot, row : row + 1] for slot in range(2)], axis=1)

    for chunk in range(chunks):
        exchange(0, chunk).start()
    for level, chunk in chunk_order(levels, chunks):
        span = slice(chunk * piece, (chunk + 1) * piece)
        bit = me // 2**level % 2
        kept = z_ref[bit, span] if level == 0 else state[level - 1, bit, span]
        exchange(level, chunk).wait_recv()
        other = taken[level, span]
        lower = jnp.where(bit == 0, kept, other)
        upper = jnp.where(bit == 0, other, kept)
        upper = permuted(upper, columns(level, 1))
        before = jnp.zeros((CROSS_SHIFT, width), jnp.float32) if chunk == 0 else previous[level]
        if chunk < chunks - 1:
            previous[level] = jnp.concatenate([before, upper], axis=0)[-CROSS_SHIFT:]
        merged = permuted(lower, columns(level, 0)) + delayed(before, upper, columns(level, 2))
        if level < levels - 1:
            state[level, 0, span] = merged[:, :rows]
            state[level, 1, span] = merged[:, rows:]
            exchange(level + 1, chunk).start()
        else:
            final[span] = merged

    final = final[...]
    centred = final - jnp.mean(final, axis=0, keepdims=True)
    boxcar = centred * lax.rsqrt(jnp.mean(centred * centred, axis=0, keepdims=True) + epsilon)
    maxima = [jnp.max(boxcar, axis=0, keepdims=True)]
    for count in range(1, WIDTHS):
        boxcar = boxcar + later(boxcar, 2 ** (count - 1))
        maxima.append(jnp.max(boxcar, axis=0, keepdims=True) / math.sqrt(2**count))
    maxima = jnp.concatenate(maxima, axis=0)
    beam = me % 2

    def send(slot):
        return pltpu.make_async_remote_copy(
            src_ref=peaks.at[slot],
            dst_ref=landed.at[beam],
            send_sem=end_send.at[slot],
            recv_sem=end_recv.at[beam],
            device_id={"freq": goals[slot]},
            device_id_type=MESH,
        )

    for slot in range(2):
        peaks[slot] = maxima[:, slot * rows : (slot + 1) * rows]
    for slot in range(2):

        @pl.when(goals[slot] != me)
        def _():
            send(slot).start()

        @pl.when(goals[slot] == me)
        def _():
            landed[beam] = peaks[slot]

    for slot in range(2):

        @pl.when(goals[slot] != me)
        def _():
            send(slot).wait_send()

    for source in range(2):

        @pl.when(origins[source] != me)
        def _():
            pltpu.make_async_remote_copy(
                src_ref=peaks.at[0],
                dst_ref=landed.at[source],
                send_sem=end_send.at[0],
                recv_sem=end_recv.at[source],
                device_id={"freq": origins[source]},
                device_id_type=MESH,
            ).wait_recv()

    out_ref[...] = landed[...]
    for level in range(levels):
        for chunk in range(chunks):
            exchange(level, chunk).wait_send()


def local(voltages, sub_delays, merge_tables):
    n = lax.axis_size("freq")
    return subbands(voltages, sub_delays, merge_tables, n)


def solution(mesh):
    return jax.shard_map(
        local,
        mesh=mesh,
        in_specs=(P(None, "beam", "freq", None, None), P("freq", None), P(None, None, "freq")),
        out_specs=P("beam", None, "freq"),
        check_vma=False,
    )
```
